128 devices in a mesh: seq: 32 (over x, y_lo, z), tp: 4 (over y_hi, core).
Axes of the slice: x: 4, y: 4 (y_hi: 2, y_lo: 2; y = y_hi * 2 + y_lo), z: 4, core: 2. Of those that a mesh axis runs over, the one named last changes fastest.
Arguments:
- query_heads: bfloat16 [8192, 2048], P('seq', 'tp'), may hold values from -96 to 96
- key_heads: bfloat16 [8192, 2048], P('seq', 'tp'), may hold values from -4 to 4
- value_heads: bfloat16 [8192, 2048], P('seq', 'tp'), may hold values from -6 to 6
- residual: bfloat16 [8192, 4096], P('seq'), may hold values from -64 to 64
- out_weight: bfloat16 [2048, 4096], P('tp'), may hold values from -0.125 to 0.125
- ln_gain: float32 [4096], replicated, may hold values from 0.1 to 1.9
- up_source: bfloat16 [4096, 4096], P(None, 'tp'), may hold values from -0.09375 to 0.09375
- down_source: bfloat16 [4096, 4096], P('tp'), may hold values from -0.09375 to 0.09375
- copy_gain: float32 [4096], P('tp'), may hold values from 0.3 to 3
- neuron_source: int32 [4096], P('tp'), may hold values from 0 to 4095, as said below
- cotangent: bfloat16 [8192, 4096], P('seq'), may hold values from -6 to 6
Outputs:
- encoded: float32 [8192, 4096], P(('seq', 'tp'))
- grad_query: float32 [8192, 2048], P('seq', 'tp')
- grad_key: float32 [8192, 2048], P('seq', 'tp')
- grad_value: float32 [8192, 2048], P('seq', 'tp')
- grad_residual: float32 [8192, 4096], P('seq', 'tp')
The draws below stay inside these ranges and needn't reach their ends.
Inputs may be any that keep to these rules, and one draw needn't show every extreme that they name: Added neuron j splits a source neuron of its own group: neuron_source[j] // 1024 == j // 1024.
All inputs are finite; a program needn't handle non-finite values.
Results may differ from the reference program's by a relative error of at most 0.035.
Values may be sent and summed in bfloat16 or wider, within the bound.
No kernel may reach another device: no remote copies, remote signals or barrier semaphores. Data moves between devices by JAX's collectives and lax.ppermute only.
A program may use at most 128 MiB of HBM per device.

```python
import math
import jax
import jax.numpy as jnp
from jax import lax

D = 4096
HEADS = 16
HEAD_DIM = 128
FF_SRC = 4096
FF_COPY = 4096
TOK_DEV = 256
TOKENS = 8192
SRC_SHARD = 1024
COPY_SHARD = 1024
N_SEQ = 32
N_TP = 4


def query_key_pair(key):
    head_width = HEADS * HEAD_DIM
    query_base = jax.random.truncated_normal(jax.random.fold_in(key, 11), -4.0, 4.0, (TOKENS, head_width), jnp.float32)
    key_base = jax.random.truncated_normal(jax.random.fold_in(key, 12), -4.0, 4.0, (TOKENS, head_width), jnp.float32)
    return (query_base, key_base)


def draw_query_heads(key, part):
    return query_key_pair(key)[0].astype(jnp.bfloat16)


def draw_key_heads(key, part):
    return query_key_pair(key)[1].astype(jnp.bfloat16)


def draw_residual(key, part):
    base = jax.random.truncated_normal(jax.random.fold_in(key, 21), -5.0, 5.0, (TOKENS, D), jnp.float32)
    column_scale = jnp.exp(jax.random.uniform(jax.random.fold_in(key, 22), (1, D), jnp.float32, math.log(0.3), math.log(3.0)))
    return (base * column_scale).astype(jnp.bfloat16)


def draw_neuron_source(key, part):
    local_pick = jax.random.randint(key, (FF_COPY,), 0, SRC_SHARD, dtype=jnp.int32)
    owner_group = jnp.arange(FF_COPY, dtype=jnp.int32) // COPY_SHARD
    picked = owner_group * SRC_SHARD + local_pick
    return picked.at[0].set(0).at[FF_COPY - 1].set(FF_SRC - 1)


def shard_levels(own_key, extent, pieces, low, largest):
    level = 1.0
    for position, parts in pieces:
        steps = jax.random.uniform(jax.random.fold_in(jax.random.fold_in(own_key, 6), position), (parts,), jnp.float32, low / len(pieces), largest / len(pieces))
        level = level * jnp.repeat(jnp.exp(steps), extent[position] // parts).reshape((-1,) + (1,) * (len(extent) - 1 - position))
    return level


def noise(own_key, dims, width, limit, cuts=(), held_as=jnp.bfloat16):
    values = jax.random.normal(own_key, dims, jnp.float32) * width
    if len(cuts) > 0:
        values = shard_levels(own_key, dims, cuts, -0.22, 0.18) * values
    return jnp.clip(values, min=-limit, max=limit).astype(held_as)


def setup_inputs(seed: int = 0) -> dict:
    seeds = jax.random.split(jax.random.key(seed), 12)
    query_heads = draw_query_heads(jax.random.fold_in(seeds[11], 71), 0)
    key_heads = draw_key_heads(jax.random.fold_in(seeds[11], 71), 0)
    value_heads = noise(seeds[2], (TOKENS, HEADS * HEAD_DIM), 1.0, 6.0, ((0, 32), (1, 4)))
    residual = draw_residual(jax.random.fold_in(seeds[11], 71), 0)
    out_weight = noise(seeds[4], (HEADS * HEAD_DIM, D), (HEADS * HEAD_DIM) ** -0.5, 0.125, ((0, 4),))
    ln_gain = jnp.clip(1.0 + 0.18 * jax.random.normal(seeds[5], (D,), jnp.float32), 0.1, 1.9)
    up_source = noise(seeds[6], (D, FF_SRC), D ** -0.5, 0.09375, ((1, 4),))
    down_source = noise(seeds[7], (FF_SRC, D), FF_SRC ** -0.5, 0.09375, ((0, 4),))
    copy_gain = jnp.clip(jnp.exp(math.log(3.0) - 2.3025851 * jax.random.uniform(seeds[8], (FF_COPY,), jnp.float32) ** shard_levels(seeds[8], (FF_COPY,), ((0, 4),), -0.2, 0.2)), 0.3, 3.0)
    neuron_source = draw_neuron_source(jax.random.fold_in(seeds[11], 71), 0)
    cotangent = noise(seeds[10], (TOKENS, D), 1.0, 6.0, ((0, 32),))
    return dict(query_heads=query_heads, key_heads=key_heads, value_heads=value_heads, residual=residual, out_weight=out_weight, ln_gain=ln_gain, up_source=up_source, down_source=down_source, copy_gain=copy_gain, neuron_source=neuron_source, cotangent=cotangent)


epsilon = 1e-05

def gelu_slope(inputs):
    output, pull_back = jax.vjp(jax.nn.gelu, inputs)
    return (output, pull_back(jnp.ones_like(inputs))[0])

def layer_norm_rows(stream):
    centered = stream - lax.optimization_barrier(jnp.mean(stream, axis=-1, keepdims=True))
    row_sigma = jnp.sqrt(lax.optimization_barrier(jnp.mean(centered * centered, axis=-1, keepdims=True)) + epsilon)
    return (centered / row_sigma, row_sigma)

def reference(query_heads, key_heads, value_heads, residual, out_weight, ln_gain, up_source, down_source, copy_gain, neuron_source, cotangent):
    head_width = HEADS * HEAD_DIM
    group_heads = head_width // N_TP
    group_src = FF_SRC // N_TP
    score_scale = 1.0 / math.sqrt(HEAD_DIM)
    margin = 2 * TOK_DEV
    span_rows = 5 * TOK_DEV

    def pad_rows(array):
        return jnp.pad(array.reshape(TOKENS, HEADS, HEAD_DIM), ((margin, margin), (0, 0), (0, 0)))
    key_pad = pad_rows(key_heads)
    value_pad = pad_rows(value_heads)

    def block_view(block):
        row_start = (block * TOK_DEV).astype(jnp.int32)
        queries = lax.dynamic_slice_in_dim(query_heads, row_start, TOK_DEV, 0).reshape(TOK_DEV, HEADS, HEAD_DIM)
        keys_near = lax.dynamic_slice_in_dim(key_pad, row_start, span_rows, 0)
        values_near = lax.dynamic_slice_in_dim(value_pad, row_start, span_rows, 0)
        block_of = block + jnp.arange(span_rows, dtype=jnp.int32) // TOK_DEV - 2
        is_valid = (block_of >= 0) & (block_of < N_SEQ)
        scores = jnp.einsum('rhd,khd->hrk', queries.astype(jnp.float32), keys_near.astype(jnp.float32)) * score_scale
        scores = jnp.where(is_valid[None, None, :], scores, -jnp.inf)
        row_top = lax.optimization_barrier(jnp.max(scores, axis=-1, keepdims=True))
        exp_scores = jnp.exp(scores - row_top)
        attn_probs = exp_scores / lax.optimization_barrier(jnp.sum(exp_scores, axis=-1, keepdims=True))
        return (row_start, queries, keys_near, values_near, attn_probs)

    def forward_block(block):
        row_start, queries, keys_near, values_near, attn_probs = block_view(block)
        attn_low = attn_probs.astype(jnp.bfloat16)
        return jnp.einsum('hrk,khd->rhd', attn_low.astype(jnp.float32), values_near.astype(jnp.float32)).astype(jnp.bfloat16)
    block_ids = jnp.arange(N_SEQ, dtype=jnp.int32)
    attended = lax.map(forward_block, block_ids).reshape(TOKENS, head_width)
    mixed = jnp.zeros((TOKENS, D), jnp.float32)
    for group_index in range(N_TP):
        head_cols = slice(group_index * group_heads, (group_index + 1) * group_heads)
        head_part = jnp.dot(attended[:, head_cols], out_weight[head_cols], preferred_element_type=jnp.float32).astype(jnp.bfloat16)
        mixed = mixed + head_part.astype(jnp.float32)
    stream = residual.astype(jnp.float32) + mixed
    unit_rows, row_sigma = layer_norm_rows(stream)
    normed_full = unit_rows * ln_gain
    normed = normed_full.astype(jnp.bfloat16)
    hidden_in = jnp.dot(normed, up_source, preferred_element_type=jnp.float32)
    counts = jnp.ones((FF_SRC,), jnp.float32).at[neuron_source].add(1.0)
    copies_in = hidden_in[:, neuron_source] * copy_gain
    act_src, slope_src = gelu_slope(hidden_in)
    act_copy, slope_copy = gelu_slope(copies_in)
    merged = (act_src.at[:, neuron_source].add(act_copy) / counts).astype(jnp.bfloat16)
    ffn_total = jnp.zeros((TOKENS, D), jnp.float32)
    for group_index in range(N_TP):
        src_cols = slice(group_index * group_src, (group_index + 1) * group_src)
        ffn_part = jnp.dot(merged[:, src_cols], down_source[src_cols], preferred_element_type=jnp.float32).astype(jnp.bfloat16)
        ffn_total = ffn_total + ffn_part.astype(jnp.float32)
    encoded = normed_full + ffn_total
    grad_merged = jnp.dot(cotangent, down_source.T, preferred_element_type=jnp.float32)
    inverse = 1.0 / counts
    grad_src = grad_merged * inverse * slope_src
    grad_copy = grad_merged[:, neuron_source] * inverse[neuron_source] * slope_copy
    grad_hidden = grad_src.at[:, neuron_source].add(grad_copy * copy_gain).astype(jnp.bfloat16)
    grad_normed = cotangent.astype(jnp.float32)
    for group_index in range(N_TP):
        src_cols = slice(group_index * group_src, (group_index + 1) * group_src)
        back_part = jnp.dot(grad_hidden[:, src_cols], up_source[:, src_cols].T, preferred_element_type=jnp.float32).astype(jnp.bfloat16)
        grad_normed = grad_normed + back_part.astype(jnp.float32)
    scaled = grad_normed * ln_gain
    grad_residual = (scaled - lax.optimization_barrier(jnp.mean(scaled, axis=-1, keepdims=True)) - unit_rows * lax.optimization_barrier(jnp.mean(scaled * unit_rows, axis=-1, keepdims=True))) / row_sigma
    grad_low = grad_residual.astype(jnp.bfloat16)
    grad_attended = jnp.dot(grad_low, out_weight.T, preferred_element_type=jnp.float32).astype(jnp.bfloat16)
    grad_start = jnp.zeros((TOKENS + 2 * margin, HEADS, HEAD_DIM), jnp.float32)

    def backward_block(carry, block):
        key_acc, value_acc = carry
        row_start, queries, keys_near, values_near, attn_probs = block_view(block)
        attn_low = attn_probs.astype(jnp.bfloat16)
        out_block = lax.dynamic_slice_in_dim(attended, row_start, TOK_DEV, 0).reshape(TOK_DEV, HEADS, HEAD_DIM)
        grad_block = lax.dynamic_slice_in_dim(grad_attended, row_start, TOK_DEV, 0).reshape(TOK_DEV, HEADS, HEAD_DIM)
        row_delta = lax.optimization_barrier(jnp.sum(grad_block.astype(jnp.float32) * out_block.astype(jnp.float32), axis=-1)).T
        grad_probs = jnp.einsum('rhd,khd->hrk', grad_block.astype(jnp.float32), values_near.astype(jnp.float32))
        grad_scores = (attn_probs * (grad_probs - row_delta[:, :, None])).astype(jnp.bfloat16)
        grad_q = score_scale * jnp.einsum('hrk,khd->rhd', grad_scores.astype(jnp.float32), keys_near.astype(jnp.float32))
        grad_k = score_scale * jnp.einsum('hrk,rhd->khd', grad_scores.astype(jnp.float32), queries.astype(jnp.float32))
        grad_v = jnp.einsum('hrk,rhd->khd', attn_low.astype(jnp.float32), grad_block.astype(jnp.float32))
        key_acc = lax.dynamic_update_slice_in_dim(key_acc, lax.dynamic_slice_in_dim(key_acc, row_start, span_rows, 0) + grad_k, row_start, 0)
        value_acc = lax.dynamic_update_slice_in_dim(value_acc, lax.dynamic_slice_in_dim(value_acc, row_start, span_rows, 0) + grad_v, row_start, 0)
        return ((key_acc, value_acc), grad_q)
    (key_acc, value_acc), grad_q = lax.scan(backward_block, (grad_start, grad_start), block_ids)
    grad_query = grad_q.reshape(TOKENS, head_width)
    grad_key = key_acc[margin:margin + TOKENS].reshape(TOKENS, head_width)
    grad_value = value_acc[margin:margin + TOKENS].reshape(TOKENS, head_width)
    return (encoded, grad_query, grad_key, grad_value, grad_residual)
```

```python
import functools
import math

import jax
import jax.numpy as jnp
from jax import lax
from jax.experimental import pallas as pl
from jax.experimental.pallas import tpu as pltpu
from jax.sharding import PartitionSpec as P

HEAD_DIM = 128
EPSILON = 1e-05
LOG2E = math.log2(math.e)
F32 = jnp.float32
BF16 = jnp.bfloat16
NT = (((1,), (1,)), ((), ()))
STAT_ROWS = 16
VMEM_LIMIT = 56 * 1024 * 1024
WEIGHT_PARTS = 8

VMEM = pl.BlockSpec(memory_space=pltpu.VMEM)
SMEM = pl.BlockSpec(memory_space=pltpu.SMEM)
ANY = pl.BlockSpec(memory_space=pl.ANY)


def call(kernel, out_shape, in_specs, scratch=(), flops=0):
    return pl.pallas_call(
        kernel,
        out_shape=out_shape,
        in_specs=in_specs,
        out_specs=jax.tree.map(lambda _: VMEM, out_shape),
        scratch_shapes=list(scratch),
        compiler_params=pltpu.CompilerParams(vmem_limit_bytes=VMEM_LIMIT),
        cost_estimate=pl.CostEstimate(flops=flops, bytes_accessed=8 << 20, transcendentals=0),
    )


def shape(dims, dtype):
    return jax.ShapeDtypeStruct(dims, dtype)


def dot(a, b):
    return jnp.dot(a, b, preferred_element_type=F32)


def dot_nt(a, b):
    return lax.dot_general(a, b, NT, preferred_element_type=F32)


def swap_core(array):
    return lax.ppermute(array, "tp", [(0, 1), (1, 0), (2, 3), (3, 2)])


def swap_chip(array):
    return lax.ppermute(array, "tp", [(0, 2), (2, 0), (1, 3), (3, 1)])


def from_behind(array, by):
    count = lax.axis_size("seq")
    return lax.ppermute(array, "seq", [(i, i + by) for i in range(count) if 0 <= i + by < count])


def three_parts(values):
    high = values.astype(BF16).astype(F32)
    middle = (values - high).astype(BF16).astype(F32)
    low = values - high - middle
    return high, middle, low


def stat_rows(columns, heads):
    rows = columns.T[:heads]
    parts = three_parts(rows)
    fill = jnp.zeros((STAT_ROWS - 3 * heads, rows.shape[1]), F32)
    return jnp.concatenate(parts + (fill,), axis=0).astype(BF16)


def read_stat(pack, head, heads, rows):
    block = pack[rows : rows + STAT_ROWS, :rows].astype(F32)
    total = block[head : head + 1]
    for part in (1, 2):
        total = total + block[part * heads + head : part * heads + head + 1]
    return total


def local_rows(ref, core, chunk, half):
    start = chunk * 2 * half
    own = ref[pl.ds(start + core * half, half)]
    other = ref[pl.ds(start + (1 - core) * half, half)]
    return own, other


def attention_kernel(scale, place, q_ref, k0, v0, kv_a, kv_b, kv_c, kv_d, att_ref, pack_ref, lse_ref):
    rows, width = q_ref.shape
    heads = width // HEAD_DIM
    half = rows // 4
    seq, blocks, core = place[0], place[1], place[2]
    for chunk in range(2):
        own, other = local_rows(q_ref, core, chunk, half)
        pack_ref[2 * chunk * half : (2 * chunk + 1) * half] = own
        pack_ref[(2 * chunk + 1) * half : (2 * chunk + 2) * half] = other
    lane = lax.broadcasted_iota(jnp.int32, (rows, HEAD_DIM), 1)
    lse_all = jnp.zeros((rows, HEAD_DIM), F32)
    for head in range(heads):
        cols = slice(head * HEAD_DIM, (head + 1) * HEAD_DIM)
        query = pack_ref[:rows, cols]
        scores = []
        values = []
        for offset, pair in ((0, None), (-2, kv_a), (-1, kv_b), (1, kv_c), (2, kv_d)):
            key = k0[:, cols] if pair is None else pair[0, :, cols]
            values.append(v0[:, cols] if pair is None else pair[1, :, cols])
            score = dot_nt(query, key) * (scale * LOG2E)
            if pair is not None:
                valid = (seq + offset >= 0) & (seq + offset < blocks)
                score = jnp.where(valid, score, -1e30)
            scores.append(score)
        top = scores[0]
        for score in scores[1:]:
            top = jnp.maximum(top, score)
        top = jnp.max(top, axis=1, keepdims=True)
        total = jnp.zeros((rows, rows), F32)
        mixed = jnp.zeros((rows, HEAD_DIM), F32)
        for score, value in zip(scores, values):
            weight = jnp.exp2(score - top)
            total = total + weight
            mixed = mixed + dot(weight.astype(BF16), value)
        total = jnp.sum(total, axis=1, keepdims=True)
        att_ref[:, cols] = (mixed / total).astype(BF16)
        lse_all = jnp.where(lane == head, top + jnp.log2(total), lse_all)
    lse_ref[...] = lse_all
    pack_ref[rows:, :rows] = stat_rows(lse_all, heads)
    pack_ref[rows:, rows:] = jnp.zeros((STAT_ROWS, width - rows), BF16)


def out_kernel(att_ref, weight_hbm, own_ref, other_ref, weight, sems):
    rows = att_ref.shape[0]
    half = rows // 4
    width = weight.shape[1]
    step = width // sems.shape[0]
    copies = []
    for part in range(sems.shape[0]):
        cols = pl.ds(part * step, step)
        copies.append(pltpu.make_async_copy(weight_hbm.at[:, cols], weight.at[:, cols], sems.at[part]))
        copies[-1].start()
    for part, copy in enumerate(copies):
        copy.wait()
        cols = slice(part * step, (part + 1) * step)
        product = dot(att_ref[...], weight[:, cols]).astype(BF16)
        for chunk in range(2):
            start = 2 * chunk * half
            own_ref[chunk, :, cols] = product[start : start + half]
            other_ref[chunk, :, cols] = product[start + half : start + 2 * half]


def norm_kernel(own_ref, far_ref, residual_ref, gain_ref, unit_ref, sigma_ref, normed_ref):
    stream = residual_ref[...].astype(F32) + own_ref[...].astype(F32) + far_ref[...].astype(F32)
    centered = stream - jnp.mean(stream, axis=-1, keepdims=True)
    sigma = jnp.sqrt(jnp.mean(centered * centered, axis=-1, keepdims=True) + EPSILON)
    unit = centered / sigma
    unit_ref[...] = unit
    sigma_ref[...] = jnp.broadcast_to(sigma, sigma_ref.shape)
    normed_ref[...] = (unit * gain_ref[...]).astype(BF16)


def norm_back_kernel(own_ref, far_ref, cot_ref, gain_ref, unit_ref, sigma_ref, low_ref):
    grad = cot_ref[...].astype(F32) + own_ref[...].astype(F32) + far_ref[...].astype(F32)
    scaled = grad * gain_ref[...]
    unit = unit_ref[...]
    mean = jnp.mean(scaled, axis=-1, keepdims=True)
    along = jnp.mean(scaled * unit, axis=-1, keepdims=True)
    low_ref[...] = ((scaled - mean - unit * along) / sigma_ref[:, :1]).astype(BF16)


def gelu_and_slope(v):
    root = math.sqrt(2.0 / math.pi)
    square = v * v
    t = jnp.tanh(v * (root + root * 0.044715 * square))
    plus = 0.5 + 0.5 * t
    slope = plus + 0.5 * v * (1.0 - t * t) * (root + 3.0 * root * 0.044715 * square)
    return v * plus, slope


def ffn_kernel(
    own_ref, near_ref, up_hbm, pick_hbm, grad_hbm, grad_copy_hbm, inverse_ref, gain_ref,
    merged_ref, back_own_ref, back_other_ref,
    up, pick, grad, grad_copy, hidden, hidden_grad, sems, side_sems,
):
    half, width = own_ref.shape
    parts = sems.shape[0]
    step = width // parts
    copies = []
    for part in range(parts):
        rows = pl.ds(part * step, step)
        copies.append(pltpu.make_async_copy(up_hbm.at[rows], up.at[rows], sems.at[part]))
        copies[-1].start()
    sides = [
        pltpu.make_async_copy(source, target, side_sems.at[i])
        for i, (source, target) in enumerate(((pick_hbm, pick), (grad_hbm, grad), (grad_copy_hbm, grad_copy)))
    ]
    for side in sides:
        side.start()
    for part, copy in enumerate(copies):
        copy.wait()
        cols = slice(part * step, (part + 1) * step)
        rows = jnp.concatenate([own_ref[:, cols], near_ref[:, cols]], axis=0)
        product = dot(rows, up[cols])
        hidden[...] = product if part == 0 else hidden[...] + product
    for side in sides:
        side.wait()
    source = hidden[...]
    high = source.astype(BF16)
    low = (source - high.astype(F32)).astype(BF16)
    copied = (dot(high, pick[...]) + dot(low, pick[...])) * gain_ref[...]
    act_copy, slope_copy = gelu_and_slope(copied)
    act, slope = gelu_and_slope(source)
    merged = act + dot_nt(act_copy.astype(BF16), pick[...])
    merged_ref[...] = (merged * inverse_ref[...]).astype(BF16)
    back_copy = (grad_copy[...] * slope_copy).astype(BF16)
    hidden_grad[...] = (grad[...] * slope + dot_nt(back_copy, pick[...])).astype(BF16)
    for part in range(parts):
        cols = slice(part * step, (part + 1) * step)
        product = dot_nt(hidden_grad[...], up[cols]).astype(BF16)
        back_own_ref[:, cols] = product[:half]
        back_other_ref[:, cols] = product[half:]


def grad_attended_kernel(own0, near0, own1, near1, weight_ref, att_ref, pack_ref, delta_ref):
    rows, width = att_ref.shape
    heads = width // HEAD_DIM
    low = jnp.concatenate([own0[...], near0[...], own1[...], near1[...]], axis=0)
    grad = dot_nt(low, weight_ref[...]).astype(BF16)
    pack_ref[:rows] = grad
    product = grad.astype(F32) * att_ref[...].astype(F32)
    lane = lax.broadcasted_iota(jnp.int32, (rows, HEAD_DIM), 1)
    delta = jnp.zeros((rows, HEAD_DIM), F32)
    for head in range(heads):
        part = jnp.sum(product[:, head * HEAD_DIM : (head + 1) * HEAD_DIM], axis=1, keepdims=True)
        delta = jnp.where(lane == head, part, delta)
    delta_ref[...] = delta
    pack_ref[rows:, :rows] = stat_rows(delta, heads)
    pack_ref[rows:, rows:] = jnp.zeros((STAT_ROWS, width - rows), BF16)


def grad_query_kernel(
    scale, place, q_pack, do_pack, lse_ref, delta_ref, k0, v0, kv_a, kv_b, kv_c, kv_d, grad_ref
):
    rows, width = grad_ref.shape
    heads = width // HEAD_DIM
    half = rows // 4
    seq, blocks, core = place[0], place[1], place[2]
    for head in range(heads):
        cols = slice(head * HEAD_DIM, (head + 1) * HEAD_DIM)
        query, out_grad = q_pack[:rows, cols], do_pack[:rows, cols]
        lse, delta = lse_ref[:, head : head + 1], delta_ref[:, head : head + 1]
        total = jnp.zeros((rows, HEAD_DIM), F32)
        for offset, pair in ((0, None), (-2, kv_a), (-1, kv_b), (1, kv_c), (2, kv_d)):
            key = k0[:, cols] if pair is None else pair[0, :, cols]
            value = v0[:, cols] if pair is None else pair[1, :, cols]
            score = dot_nt(query, key) * (scale * LOG2E) - lse
            if pair is not None:
                valid = (seq + offset >= 0) & (seq + offset < blocks)
                score = jnp.where(valid, score, -1e30)
            grad_score = jnp.exp2(score) * (dot_nt(out_grad, value) - delta)
            total = total + dot(grad_score.astype(BF16), key)
        total = total * scale
        for chunk in range(2):
            start = 2 * chunk * half
            grad_ref[pl.ds(start + core * half, half), cols] = total[start : start + half]
            grad_ref[pl.ds(start + (1 - core) * half, half), cols] = total[start + half : start + 2 * half]


def grad_key_value_kernel(scale, count, start, *refs):
    packs, refs = refs[: 2 * count], refs[2 * count :]
    k0, v0 = refs[:2]
    grad_key_ref, grad_value_ref = refs[-2:]
    rows, width = k0.shape
    heads = width // HEAD_DIM
    for head in range(heads):
        cols = slice(head * HEAD_DIM, (head + 1) * HEAD_DIM)
        key, value = k0[:, cols], v0[:, cols]
        grad_key = jnp.zeros((rows, HEAD_DIM), F32)
        grad_value = jnp.zeros((rows, HEAD_DIM), F32)
        for index in range(count):
            q_pack, do_pack = packs[2 * index], packs[2 * index + 1]
            query, out_grad = q_pack[:rows, cols], do_pack[:rows, cols]
            score = dot_nt(key, query) * (scale * LOG2E) - read_stat(q_pack, head, heads, rows)
            weight = jnp.exp2(score)
            grad_value = grad_value + dot(weight.astype(BF16), out_grad)
            grad_score = weight * (dot_nt(value, out_grad) - read_stat(do_pack, head, heads, rows))
            grad_key = grad_key + dot(grad_score.astype(BF16), query)
        grad_key = grad_key * scale
        if not start:
            grad_key = grad_key + refs[2][:, cols]
            grad_value = grad_value + refs[3][:, cols]
        grad_key_ref[:, cols] = grad_key
        grad_value_ref[:, cols] = grad_value


def shards(
    query_heads,
    key_heads,
    value_heads,
    residual,
    out_weight,
    ln_gain,
    up_source,
    down_source,
    copy_gain,
    neuron_source,
    cotangent,
):
    rows, head_width = query_heads.shape
    model_width = residual.shape[1]
    src_width = up_source.shape[1]
    half = rows // 4
    scale = 1.0 / math.sqrt(HEAD_DIM)
    seq = lax.axis_index("seq")
    blocks = lax.axis_size("seq")
    tp_place = lax.axis_index("tp")
    core, chip = tp_place % 2, tp_place // 2
    place = jnp.stack([seq, jnp.full_like(seq, blocks), core]).astype(jnp.int32)

    kv = jnp.stack([key_heads, value_heads])
    behind1 = from_behind(kv, 1)
    ahead1 = from_behind(kv, -1)
    behind2 = from_behind(behind1, 1)
    ahead2 = from_behind(ahead1, -1)
    window = (key_heads, value_heads, behind2, behind1, ahead1, ahead2)

    def own_rows(array):
        split = array.reshape(2, 2, half, array.shape[1])
        return lax.dynamic_slice_in_dim(split, core, 1, 1)[:, 0]

    def other_rows(array):
        split = array.reshape(2, 2, half, array.shape[1])
        return lax.dynamic_slice_in_dim(split, 1 - core, 1, 1)[:, 0]

    residual_own = own_rows(residual)
    cot_own = own_rows(cotangent)
    cot_local = jnp.stack([cot_own, other_rows(cotangent)], axis=1)
    local_source = neuron_source - tp_place * src_width
    pick = (lax.broadcasted_iota(jnp.int32, (src_width, src_width), 0) == local_source[None, :])
    counts = 1.0 + jnp.sum(pick.astype(F32), axis=1)
    pick = pick.astype(BF16)
    inverse = 1.0 / counts
    grad_merged = dot_nt(cot_local.reshape(rows, model_width), down_source) * inverse
    grad_high = grad_merged.astype(BF16)
    grad_low = (grad_merged - grad_high.astype(F32)).astype(BF16)
    grad_copy = (dot(grad_high, pick) + dot(grad_low, pick)) * copy_gain
    gain_row = ln_gain.reshape(1, model_width)
    inverse_row = inverse.reshape(1, src_width)
    copy_row = copy_gain.reshape(1, src_width)

    attended, q_pack, lse = call(
        functools.partial(attention_kernel, scale),
        (
            shape((rows, head_width), BF16),
            shape((rows + STAT_ROWS, head_width), BF16),
            shape((rows, HEAD_DIM), F32),
        ),
        [SMEM] + [VMEM] * 7,
        flops=2 * 2 * rows * 5 * rows * head_width,
    )(place, query_heads, *window)

    own_part, other_part = call(
        out_kernel,
        (shape((2, half, model_width), BF16),) * 2,
        [VMEM, ANY],
        scratch=[pltpu.VMEM(out_weight.shape, BF16), pltpu.SemaphoreType.DMA((4,))],
        flops=2 * rows * head_width * model_width,
    )(attended, out_weight)
    near_part = swap_core(other_part)
    chip_sums = [(own_part[k].astype(F32) + near_part[k].astype(F32)).astype(BF16) for k in range(2)]
    far_sums = [swap_chip(chip_sum) for chip_sum in chip_sums]

    q_packs = {offset: from_behind(q_pack, -offset) for offset in (-1, 1, -2, 2)}

    units, sigmas, merges, backs = [], [], [], []
    for k in range(2):
        unit, sigma, normed = call(
            norm_kernel,
            (
                shape((half, model_width), F32),
                shape((half, HEAD_DIM), F32),
                shape((half, model_width), BF16),
            ),
            [VMEM] * 4,
        )(chip_sums[k], far_sums[k], residual_own[k], gain_row)
        near_normed = swap_core(normed)
        merged, back_own, back_other = call(
            ffn_kernel,
            (
                shape((2 * half, src_width), BF16),
                shape((half, model_width), BF16),
                shape((half, model_width), BF16),
            ),
            [VMEM, VMEM, ANY, ANY, ANY, ANY, VMEM, VMEM],
            scratch=[
                pltpu.VMEM(up_source.shape, BF16),
                pltpu.VMEM(pick.shape, BF16),
                pltpu.VMEM((2 * half, src_width), F32),
                pltpu.VMEM((2 * half, src_width), F32),
                pltpu.VMEM((2 * half, src_width), F32),
                pltpu.VMEM((2 * half, src_width), BF16),
                pltpu.SemaphoreType.DMA((WEIGHT_PARTS,)),
                pltpu.SemaphoreType.DMA((3,)),
            ],
            flops=4 * 2 * half * model_width * src_width,
        )(
            normed,
            near_normed,
            up_source,
            pick,
            grad_merged[2 * k * half : 2 * (k + 1) * half],
            grad_copy[2 * k * half : 2 * (k + 1) * half],
            inverse_row,
            copy_row,
        )
        back_near = swap_core(back_other)
        back_sum = (back_own.astype(F32) + back_near.astype(F32)).astype(BF16)
        units.append(unit)
        sigmas.append(sigma)
        merges.append(merged)
        backs.append((back_sum, swap_chip(back_sum)))

    lows, near_lows = [], []
    for k in range(2):
        low = call(norm_back_kernel, shape((half, model_width), BF16), [VMEM] * 6)(
            *backs[k], cot_own[k], gain_row, units[k], sigmas[k]
        )
        lows.append(low)
        near_lows.append(swap_core(low))

    do_pack, delta = call(
        grad_attended_kernel,
        (shape((rows + STAT_ROWS, head_width), BF16), shape((rows, HEAD_DIM), F32)),
        [VMEM] * 6,
        flops=2 * rows * head_width * model_width,
    )(lows[0], near_lows[0], lows[1], near_lows[1], out_weight, attended)

    do_packs = {-1: from_behind(do_pack, 1), 1: from_behind(do_pack, -1)}
    do_packs[-2] = from_behind(do_packs[-1], 1)
    do_packs[2] = from_behind(do_packs[1], -1)

    grad_query = call(
        functools.partial(grad_query_kernel, scale),
        shape((rows, head_width), F32),
        [SMEM] + [VMEM] * 10,
        flops=3 * 2 * rows * 5 * rows * head_width,
    )(place, q_pack, do_pack, lse, delta, *window)

    def grad_key_value(pairs, sums):
        return call(
            functools.partial(grad_key_value_kernel, scale, len(pairs), not sums),
            (shape((rows, head_width), F32),) * 2,
            [VMEM] * (2 * len(pairs) + 2 + len(sums)),
            flops=len(pairs) * 4 * 2 * rows * rows * head_width,
        )(*[pack for pair in pairs for pack in pair], key_heads, value_heads, *sums)

    sums = grad_key_value([(q_pack, do_pack)], ())
    sums = grad_key_value([(q_packs[offset], do_packs[offset]) for offset in (-1, 1)], sums)
    grad_key, grad_value = grad_key_value(
        [(q_packs[offset], do_packs[offset]) for offset in (-2, 2)], sums
    )

    ffn_part = dot(jnp.concatenate(merges, axis=0), down_source).astype(BF16)
    ffn_split = ffn_part.reshape(2, 2, half, model_width)
    ffn_near = swap_core(ffn_split[:, 1])
    ffn_chip = ffn_split[:, 0].astype(F32) + ffn_near.astype(F32)
    ffn_send = jnp.where(chip == 0, ffn_chip[1], ffn_chip[0]).astype(BF16)
    ffn_far = swap_chip(ffn_send)
    ffn_mine = jnp.where(chip == 0, ffn_chip[0], ffn_chip[1])
    own_unit = jnp.where(chip == 0, units[0], units[1])
    encoded = own_unit * ln_gain + (ffn_mine + ffn_far.astype(F32))

    col_width = model_width // lax.axis_size("tp")
    low_blocks = []
    for k in range(2):
        first = jnp.where(core == 0, lows[k], near_lows[k])
        second = jnp.where(core == 0, near_lows[k], lows[k])
        low_blocks += [first, second]
    low_all = jnp.concatenate(low_blocks, axis=0)
    grad_residual = lax.dynamic_slice_in_dim(low_all, tp_place * col_width, col_width, 1).astype(F32)
    return (encoded, grad_query, grad_key, grad_value, grad_residual)


def solution(mesh):
    in_specs = (
        P("seq", "tp"),
        P("seq", "tp"),
        P("seq", "tp"),
        P("seq", None),
        P("tp", None),
        P(),
        P(None, "tp"),
        P("tp", None),
        P("tp"),
        P("tp"),
        P("seq", None),
    )
    out_specs = (
        P(("seq", "tp"), None),
        P("seq", "tp"),
        P("seq", "tp"),
        P("seq", "tp"),
        P("seq", "tp"),
    )
    return jax.shard_map(shards, mesh=mesh, in_specs=in_specs, out_specs=out_specs, check_vma=False)
```

```python
import functools
import math

import jax
import jax.numpy as jnp
from jax import lax
from jax.experimental import pallas as pl
from jax.experimental.pallas import tpu as pltpu
from jax.sharding import PartitionSpec as P

HEAD_DIM = 128
EPSILON = 1e-05
LOG2E = math.log2(math.e)
F32 = jnp.float32
BF16 = jnp.bfloat16
NT = (((1,), (1,)), ((), ()))
STAT_ROWS = 16
VMEM_LIMIT = 16 * 1024 * 1024
OUT_STEP = 512
NORM_STEP = 512
COST = 1024

VMEM = pl.BlockSpec(memory_space=pltpu.VMEM)
SMEM = pl.BlockSpec(memory_space=pltpu.SMEM)
ANY = pl.BlockSpec(memory_space=pl.ANY)


def call(kernel, out_shape, in_specs, scratch=()):
    return pl.pallas_call(
        kernel,
        out_shape=out_shape,
        in_specs=in_specs,
        out_specs=jax.tree.map(lambda _: VMEM, out_shape),
        scratch_shapes=list(scratch),
        compiler_params=pltpu.CompilerParams(vmem_limit_bytes=VMEM_LIMIT),
        cost_estimate=pl.CostEstimate(flops=COST, bytes_accessed=COST, transcendentals=0),
    )


def shape(dims, dtype):
    return jax.ShapeDtypeStruct(dims, dtype)


def dot(a, b):
    return jnp.dot(a, b, preferred_element_type=F32)


def dot_nt(a, b):
    return lax.dot_general(a, b, NT, preferred_element_type=F32)


def swap_core(array):
    return lax.ppermute(array, "tp", [(0, 1), (1, 0), (2, 3), (3, 2)])


def swap_chip(array):
    return lax.ppermute(array, "tp", [(0, 2), (2, 0), (1, 3), (3, 1)])


def after(value, *earlier):
    return lax.optimization_barrier((value, earlier))[0]


def from_behind(array, by):
    count = lax.axis_size("seq")
    return lax.ppermute(array, "seq", [(i, i + by) for i in range(count) if 0 <= i + by < count])


def three_parts(values):
    high = values.astype(BF16).astype(F32)
    middle = (values - high).astype(BF16).astype(F32)
    low = values - high - middle
    return high, middle, low


def stat_rows(columns, heads):
    rows = columns.T[:heads]
    parts = three_parts(rows)
    fill = jnp.zeros((STAT_ROWS - 3 * heads, rows.shape[1]), F32)
    return jnp.concatenate(parts + (fill,), axis=0).astype(BF16)


def read_stat(pack, head, heads, rows):
    block = pack[rows : rows + STAT_ROWS, :rows].astype(F32)
    total = block[head : head + 1]
    for part in (1, 2):
        total = total + block[part * heads + head : part * heads + head + 1]
    return total


def local_starts(core, rows):
    slab = rows // 4
    return [(2 * part + (core if own else 1 - core)) * slab for own in (True, False) for part in range(2)]


def attention_kernel(scale, place, q_ref, k0, v0, kv_a, kv_b, kv_c, kv_d, att_ref, pack_ref, lse_ref):
    rows, width = q_ref.shape
    heads = width // HEAD_DIM
    slab = rows // 4
    seq, blocks, core = place[0], place[1], place[2]
    for index, start in enumerate(local_starts(core, rows)):
        pack_ref[index * slab : (index + 1) * slab] = q_ref[pl.ds(start, slab)]
    lane = lax.broadcasted_iota(jnp.int32, (rows, HEAD_DIM), 1)
    lse_all = jnp.zeros((rows, HEAD_DIM), F32)
    for head in range(heads):
        cols = slice(head * HEAD_DIM, (head + 1) * HEAD_DIM)
        query = pack_ref[:rows, cols]
        scores = []
        values = []
        for offset, pair in ((0, None), (-2, kv_a), (-1, kv_b), (1, kv_c), (2, kv_d)):
            key = k0[:, cols] if pair is None else pair[0, :, cols]
            values.append(v0[:, cols] if pair is None else pair[1, :, cols])
            score = dot_nt(query, key) * (scale * LOG2E)
            if pair is not None:
                valid = (seq + offset >= 0) & (seq + offset < blocks)
                score = jnp.where(valid, score, -1e30)
            scores.append(score)
        top = scores[0]
        for score in scores[1:]:
            top = jnp.maximum(top, score)
        top = jnp.max(top, axis=1, keepdims=True)
        total = jnp.zeros((rows, rows), F32)
        mixed = jnp.zeros((rows, HEAD_DIM), F32)
        for score, value in zip(scores, values):
            weight = jnp.exp2(score - top)
            total = total + weight
            mixed = mixed + dot(weight.astype(BF16), value)
        total = jnp.sum(total, axis=1, keepdims=True)
        att_ref[:, cols] = (mixed / total).astype(BF16)
        lse_all = jnp.where(lane == head, top + jnp.log2(total), lse_all)
    lse_ref[...] = lse_all
    pack_ref[rows:, :rows] = stat_rows(lse_all, heads)
    pack_ref[rows:, rows:] = jnp.zeros((STAT_ROWS, width - rows), BF16)


def out_kernel(att_ref, weight_ref, own_ref, other_ref):
    rows, width = own_ref.shape
    for start in range(0, width, OUT_STEP):
        product = dot(att_ref[...], weight_ref[:, start : start + OUT_STEP]).astype(BF16)
        own_ref[:, start : start + OUT_STEP] = product[:rows]
        other_ref[:, start : start + OUT_STEP] = product[rows:]


def lane_sums(values):
    total = values[:, :HEAD_DIM]
    for start in range(HEAD_DIM, values.shape[1], HEAD_DIM):
        total = total + values[:, start : start + HEAD_DIM]
    return total


def norm_kernel(near_ref, far_ref, residual_ref, gain_ref, unit_ref, sigma_ref, normed_ref):
    rows, width = residual_ref.shape
    spans = [slice(at, at + NORM_STEP) for at in range(0, width, NORM_STEP)]
    total = jnp.zeros((rows, HEAD_DIM), F32)
    for cols in spans:
        stream = residual_ref[:, cols].astype(F32) + near_ref[:, cols].astype(F32) + far_ref[:, cols].astype(F32)
        unit_ref[:, cols] = stream
        total = total + lane_sums(stream)
    mean = jnp.sum(total, axis=-1, keepdims=True) / width
    total = jnp.zeros((rows, HEAD_DIM), F32)
    for cols in spans:
        centered = unit_ref[:, cols] - mean
        total = total + lane_sums(centered * centered)
    sigma = jnp.sqrt(jnp.sum(total, axis=-1, keepdims=True) / width + EPSILON)
    sigma_ref[...] = jnp.broadcast_to(sigma, sigma_ref.shape)
    inverse = 1.0 / sigma
    for cols in spans:
        unit = (unit_ref[:, cols] - mean) * inverse
        unit_ref[:, cols] = unit
        normed_ref[:, cols] = (unit * gain_ref[:, cols]).astype(BF16)


def norm_back_kernel(near_ref, far_ref, cot_ref, gain_ref, unit_ref, sigma_ref, low_ref, scaled_ref):
    rows, width = cot_ref.shape
    spans = [slice(at, at + NORM_STEP) for at in range(0, width, NORM_STEP)]
    total = jnp.zeros((rows, HEAD_DIM), F32)
    total_along = jnp.zeros((rows, HEAD_DIM), F32)
    for cols in spans:
        grad = cot_ref[:, cols].astype(F32) + near_ref[:, cols].astype(F32) + far_ref[:, cols].astype(F32)
        scaled = grad * gain_ref[:, cols]
        scaled_ref[:, cols] = scaled
        total = total + lane_sums(scaled)
        total_along = total_along + lane_sums(scaled * unit_ref[:, cols])
    mean = jnp.sum(total, axis=-1, keepdims=True) / width
    along = jnp.sum(total_along, axis=-1, keepdims=True) / width
    inverse = 1.0 / sigma_ref[:, :1]
    for cols in spans:
        grad = (scaled_ref[:, cols] - mean - unit_ref[:, cols] * along) * inverse
        low_ref[:, cols] = grad.astype(BF16)


def gelu_and_slope(v):
    root = math.sqrt(2.0 / math.pi)
    square = v * v
    t = jnp.tanh(v * (root + root * 0.044715 * square))
    plus = 0.5 + 0.5 * t
    slope = plus + 0.5 * v * (1.0 - t * t) * (root + 3.0 * root * 0.044715 * square)
    return v * plus, slope


def ffn_kernel(
    own_ref, near_ref, up_ref, pick_ref, grad_ref, grad_copy_ref, inverse_ref, gain_ref, merged_ref, hidden_grad_ref
):
    rows = jnp.concatenate([own_ref[...], near_ref[...]], axis=0)
    source = dot(rows, up_ref[...])
    high = source.astype(BF16)
    low = (source - high.astype(F32)).astype(BF16)
    copied = (dot(high, pick_ref[...]) + dot(low, pick_ref[...])) * gain_ref[...]
    act_copy, slope_copy = gelu_and_slope(copied)
    act, slope = gelu_and_slope(source)
    back_copy = (grad_copy_ref[...] * slope_copy).astype(BF16)
    hidden_grad_ref[...] = (grad_ref[...] * slope + dot_nt(back_copy, pick_ref[...])).astype(BF16)
    merged = act + dot_nt(act_copy.astype(BF16), pick_ref[...])
    merged_ref[...] = (merged * inverse_ref[...]).astype(BF16)


def back_kernel(hidden_grad_ref, up_ref, own_ref, other_ref):
    rows, width = own_ref.shape
    for start in range(0, width, OUT_STEP):
        product = dot_nt(hidden_grad_ref[...], up_ref[start : start + OUT_STEP]).astype(BF16)
        own_ref[:, start : start + OUT_STEP] = product[:rows]
        other_ref[:, start : start + OUT_STEP] = product[rows:]


def grad_attended_kernel(own_ref, near_ref, weight_ref, att_ref, pack_ref, delta_ref):
    rows, width = att_ref.shape
    heads = width // HEAD_DIM
    low = jnp.concatenate([own_ref[...], near_ref[...]], axis=0)
    pack_ref[:rows] = dot_nt(low, weight_ref[...]).astype(BF16)
    product = pack_ref[:rows].astype(F32) * att_ref[...].astype(F32)
    lane = lax.broadcasted_iota(jnp.int32, (rows, HEAD_DIM), 1)
    delta = jnp.zeros((rows, HEAD_DIM), F32)
    for head in range(heads):
        part = jnp.sum(product[:, head * HEAD_DIM : (head + 1) * HEAD_DIM], axis=1, keepdims=True)
        delta = jnp.where(lane == head, part, delta)
    delta_ref[...] = delta
    pack_ref[rows:, :rows] = stat_rows(delta, heads)
    pack_ref[rows:, rows:] = jnp.zeros((STAT_ROWS, width - rows), BF16)


def grad_query_kernel(
    scale, place, q_pack, do_pack, lse_ref, delta_ref, k0, v0, kv_a, kv_b, kv_c, kv_d, grad_ref
):
    rows, width = grad_ref.shape
    heads = width // HEAD_DIM
    slab = rows // 4
    seq, blocks, core = place[0], place[1], place[2]
    for head in range(heads):
        cols = slice(head * HEAD_DIM, (head + 1) * HEAD_DIM)
        query, out_grad = q_pack[:rows, cols], do_pack[:rows, cols]
        lse, delta = lse_ref[:, head : head + 1], delta_ref[:, head : head + 1]
        total = jnp.zeros((rows, HEAD_DIM), F32)
        for offset, pair in ((0, None), (-2, kv_a), (-1, kv_b), (1, kv_c), (2, kv_d)):
            key = k0[:, cols] if pair is None else pair[0, :, cols]
            value = v0[:, cols] if pair is None else pair[1, :, cols]
            score = dot_nt(query, key) * (scale * LOG2E) - lse
            if pair is not None:
                valid = (seq + offset >= 0) & (seq + offset < blocks)
                score = jnp.where(valid, score, -1e30)
            grad_score = jnp.exp2(score) * (dot_nt(out_grad, value) - delta)
            total = total + dot(grad_score.astype(BF16), key)
        total = total * scale
        for index, start in enumerate(local_starts(core, rows)):
            grad_ref[pl.ds(start, slab), cols] = total[index * slab : (index + 1) * slab]


def grad_key_value_kernel(scale, count, start, *refs):
    packs, refs = refs[: 2 * count], refs[2 * count :]
    k0, v0 = refs[:2]
    grad_key_ref, grad_value_ref = refs[-2:]
    rows, width = k0.shape
    heads = width // HEAD_DIM
    for head in range(heads):
        cols = slice(head * HEAD_DIM, (head + 1) * HEAD_DIM)
        key, value = k0[:, cols], v0[:, cols]
        grad_key = jnp.zeros((rows, HEAD_DIM), F32)
        grad_value = jnp.zeros((rows, HEAD_DIM), F32)
        for index in range(count):
            q_pack, do_pack = packs[2 * index], packs[2 * index + 1]
            query, out_grad = q_pack[:rows, cols], do_pack[:rows, cols]
            score = dot_nt(key, query) * (scale * LOG2E) - read_stat(q_pack, head, heads, rows)
            weight = jnp.exp2(score)
            grad_value = grad_value + dot(weight.astype(BF16), out_grad)
            grad_score = weight * (dot_nt(value, out_grad) - read_stat(do_pack, head, heads, rows))
            grad_key = grad_key + dot(grad_score.astype(BF16), query)
        grad_key = grad_key * scale
        if not start:
            grad_key = grad_key + refs[2][:, cols]
            grad_value = grad_value + refs[3][:, cols]
        grad_key_ref[:, cols] = grad_key
        grad_value_ref[:, cols] = grad_value


def shards(
    query_heads,
    key_heads,
    value_heads,
    residual,
    out_weight,
    ln_gain,
    up_source,
    down_source,
    copy_gain,
    neuron_source,
    cotangent,
):
    rows, head_width = query_heads.shape
    model_width = residual.shape[1]
    src_width = up_source.shape[1]
    half = rows // 2
    scale = 1.0 / math.sqrt(HEAD_DIM)
    seq = lax.axis_index("seq")
    blocks = lax.axis_size("seq")
    tp_place = lax.axis_index("tp")
    core, chip = tp_place % 2, tp_place // 2
    place = jnp.stack([seq, jnp.full_like(seq, blocks), core]).astype(jnp.int32)

    kv = jnp.stack([key_heads, value_heads])
    behind1 = from_behind(kv, 1)
    ahead1 = from_behind(kv, -1)

    def half_rows(array, place):
        split = array.reshape(2, 2, half // 2, array.shape[1])
        return lax.dynamic_slice_in_dim(split, place, 1, 1).reshape(half, array.shape[1])

    cot_own = half_rows(cotangent, core)
    cot_local = jnp.concatenate([cot_own, half_rows(cotangent, 1 - core)], axis=0)
    grad_merged = dot_nt(cot_local, down_source)
    behind1, ahead1, grad_merged = lax.optimization_barrier((behind1, ahead1, grad_merged))
    behind2 = from_behind(behind1, 1)
    ahead2 = from_behind(ahead1, -1)

    residual_own = half_rows(residual, core)
    local_source = neuron_source - tp_place * src_width
    pick = (lax.broadcasted_iota(jnp.int32, (src_width, src_width), 0) == local_source[None, :])
    counts = 1.0 + jnp.sum(pick.astype(F32), axis=1)
    pick = pick.astype(BF16)
    inverse = 1.0 / counts
    grad_merged = grad_merged * inverse
    grad_high = grad_merged.astype(BF16)
    grad_rest = (grad_merged - grad_high.astype(F32)).astype(BF16)
    grad_copy = (dot(grad_high, pick) + dot(grad_rest, pick)) * copy_gain
    gain_row = ln_gain.reshape(1, model_width)
    inverse_row = inverse.reshape(1, src_width)
    copy_row = copy_gain.reshape(1, src_width)
    behind2, ahead2, pick, grad_merged, grad_copy, residual_own = lax.optimization_barrier(
        (behind2, ahead2, pick, grad_merged, grad_copy, residual_own)
    )
    window = (key_heads, value_heads, behind2, behind1, ahead1, ahead2)

    attended, q_pack, lse = call(
        functools.partial(attention_kernel, scale),
        (
            shape((rows, head_width), BF16),
            shape((rows + STAT_ROWS, head_width), BF16),
            shape((rows, HEAD_DIM), F32),
        ),
        [SMEM] + [VMEM] * 7,
    )(place, query_heads, *window)

    def chip_sum(kernel, operands, beside):
        own, other = call(kernel, (shape((half, model_width), BF16),) * 2, [VMEM, VMEM])(*operands)
        other, beside = lax.optimization_barrier((swap_core(other), beside))
        near = (own.astype(F32) + other.astype(F32)).astype(BF16)
        return near, swap_chip(near), beside

    near, far, _ = chip_sum(out_kernel, (attended, out_weight), ())

    q_early = after(q_pack, near)
    q_packs = {offset: from_behind(q_early, -offset) for offset in (-1, 1, -2, 2)}
    far, q_packs = lax.optimization_barrier((far, q_packs))

    unit, sigma, normed = call(
        norm_kernel,
        (
            shape((half, model_width), F32),
            shape((half, HEAD_DIM), F32),
            shape((half, model_width), BF16),
        ),
        [VMEM] * 4,
    )(near, far, residual_own, gain_row)
    near_normed = swap_core(normed)
    merged, hidden_grad = call(ffn_kernel, (shape((rows, src_width), BF16),) * 2, [VMEM] * 8)(
        normed, near_normed, up_source, pick, grad_merged, grad_copy, inverse_row, copy_row
    )
    ffn_part = dot(merged, down_source).astype(BF16)
    near, far, ffn_part = chip_sum(back_kernel, (hidden_grad, up_source), ffn_part)
    ffn_near = swap_core(ffn_part[half:])
    ffn_chip = (ffn_part[:half].astype(F32) + ffn_near.astype(F32)).reshape(2, half // 2, model_width)
    ffn_send = jnp.where(chip == 0, ffn_chip[1], ffn_chip[0]).astype(BF16)
    ffn_mine = jnp.where(chip == 0, ffn_chip[0], ffn_chip[1])
    far, ffn_send, ffn_mine = lax.optimization_barrier((far, ffn_send, ffn_mine))

    low = call(
        norm_back_kernel,
        shape((half, model_width), BF16),
        [VMEM] * 6,
        scratch=[pltpu.VMEM((half, model_width), F32)],
    )(near, far, cot_own, gain_row, unit, sigma)
    near_low = swap_core(low)
    do_pack, delta = call(
        grad_attended_kernel,
        (shape((rows + STAT_ROWS, head_width), BF16), shape((rows, HEAD_DIM), F32)),
        [VMEM] * 4,
    )(low, near_low, out_weight, attended)

    do_packs = {offset: from_behind(do_pack, -offset) for offset in (-2, 2, -1, 1)}

    ffn_far = swap_chip(after(ffn_send, do_pack))

    grad_query = call(
        functools.partial(grad_query_kernel, scale),
        shape((rows, head_width), F32),
        [SMEM] + [VMEM] * 10,
    )(place, q_pack, do_pack, lse, delta, *window)

    def grad_key_value(pairs, sums):
        return call(
            functools.partial(grad_key_value_kernel, scale, len(pairs), not sums),
            (shape((rows, head_width), F32),) * 2,
            [VMEM] * (2 * len(pairs) + 2 + len(sums)),
        )(*[pack for pair in pairs for pack in pair], key_heads, value_heads, *sums)

    sums = grad_key_value(
        [(q_pack, do_pack)] + [(q_packs[offset], do_packs[offset]) for offset in (-1, 1)], ()
    )
    own_unit = lax.dynamic_slice_in_dim(unit, chip * (half // 2), half // 2, 0)
    encoded = own_unit * ln_gain + (ffn_mine + ffn_far.astype(F32))
    far_pairs = [(q_packs[offset], do_packs[offset]) for offset in (-2, 2)]
    grad_key, grad_value = grad_key_value(far_pairs, sums)

    col_width = model_width // lax.axis_size("tp")
    first = jnp.where(core == 0, low, near_low).reshape(2, half // 2, model_width)
    second = jnp.where(core == 0, near_low, low).reshape(2, half // 2, model_width)
    low_all = jnp.stack([first, second], axis=1).reshape(rows, model_width)
    grad_residual = lax.dynamic_slice_in_dim(low_all, tp_place * col_width, col_width, 1).astype(F32)
    return (encoded, grad_query, grad_key, grad_value, grad_residual)


def solution(mesh):
    in_specs = (
        P("seq", "tp"),
        P("seq", "tp"),
        P("seq", "tp"),
        P("seq", None),
        P("tp", None),
        P(),
        P(None, "tp"),
        P("tp", None),
        P("tp"),
        P("tp"),
        P("seq", None),
    )
    out_specs = (
        P(("seq", "tp"), None),
        P("seq", "tp"),
        P("seq", "tp"),
        P("seq", "tp"),
        P("seq", "tp"),
    )
    return jax.shard_map(shards, mesh=mesh, in_specs=in_specs, out_specs=out_specs, check_vma=False)
```

```python
import functools
import math

import jax
import jax.numpy as jnp
from jax import lax
from jax.experimental import pallas as pl
from jax.experimental.pallas import tpu as pltpu
from jax.sharding import PartitionSpec as P

HEAD_DIM = 128
EPSILON = 1e-05
LOG2E = math.log2(math.e)
F32 = jnp.float32
BF16 = jnp.bfloat16
NT = (((1,), (1,)), ((), ()))
STAT_ROWS = 16
VMEM_LIMIT = 16 * 1024 * 1024
OUT_STEP = 512
NORM_STEP = 512
COST = 1024

VMEM = pl.BlockSpec(memory_space=pltpu.VMEM)
SMEM = pl.BlockSpec(memory_space=pltpu.SMEM)
ANY = pl.BlockSpec(memory_space=pl.ANY)


def call(kernel, out_shape, in_specs, scratch=()):
    return pl.pallas_call(
        kernel,
        out_shape=out_shape,
        in_specs=in_specs,
        out_specs=jax.tree.map(lambda _: VMEM, out_shape),
        scratch_shapes=list(scratch),
        compiler_params=pltpu.CompilerParams(vmem_limit_bytes=VMEM_LIMIT),
        cost_estimate=pl.CostEstimate(flops=COST, bytes_accessed=COST, transcendentals=0),
    )


def shape(dims, dtype):
    return jax.ShapeDtypeStruct(dims, dtype)


def dot(a, b):
    return jnp.dot(a, b, preferred_element_type=F32)


def dot_nt(a, b):
    return lax.dot_general(a, b, NT, preferred_element_type=F32)


def swap_core(array):
    return lax.ppermute(array, "tp", [(0, 1), (1, 0), (2, 3), (3, 2)])


def swap_chip(array):
    return lax.ppermute(array, "tp", [(0, 2), (2, 0), (1, 3), (3, 1)])


def after(value, *earlier):
    return lax.optimization_barrier((value, earlier))[0]


def swap_block(array, first):
    count = lax.axis_size("seq")
    ahead = [(i, i + 1) for i in range(first, count - 1, 2)]
    return lax.ppermute(array, "seq", ahead + [(j, i) for i, j in ahead])


def nearby_offsets(seq):
    side = 1 - 2 * (seq % 2)
    return side, -side, 2 * side, -2 * side


def three_parts(values):
    high = values.astype(BF16).astype(F32)
    middle = (values - high).astype(BF16).astype(F32)
    low = values - high - middle
    return high, middle, low


def stat_rows(columns, heads):
    rows = columns.T[:heads]
    parts = three_parts(rows)
    fill = jnp.zeros((STAT_ROWS - 3 * heads, rows.shape[1]), F32)
    return jnp.concatenate(parts + (fill,), axis=0).astype(BF16)


def read_stat(pack, head, heads, rows):
    block = pack[rows : rows + STAT_ROWS, :rows].astype(F32)
    total = block[head : head + 1]
    for part in (1, 2):
        total = total + block[part * heads + head : part * heads + head + 1]
    return total


def local_starts(core, rows):
    slab = rows // 4
    return [(2 * part + (core if own else 1 - core)) * slab for own in (True, False) for part in range(2)]


def attention_kernel(scale, place, q_ref, k0, v0, kv_a, kv_b, kv_c, kv_d, att_ref, pack_ref, lse_ref):
    rows, width = q_ref.shape
    heads = width // HEAD_DIM
    slab = rows // 4
    seq, blocks, core = place[0], place[1], place[2]
    for index, start in enumerate(local_starts(core, rows)):
        pack_ref[index * slab : (index + 1) * slab] = q_ref[pl.ds(start, slab)]
    lane = lax.broadcasted_iota(jnp.int32, (rows, HEAD_DIM), 1)
    lse_all = jnp.zeros((rows, HEAD_DIM), F32)
    for head in range(heads):
        cols = slice(head * HEAD_DIM, (head + 1) * HEAD_DIM)
        query = pack_ref[:rows, cols]
        scores = []
        values = []
        for offset, pair in zip((0,) + nearby_offsets(seq), (None, kv_a, kv_b, kv_c, kv_d)):
            key = k0[:, cols] if pair is None else pair[0, :, cols]
            values.append(v0[:, cols] if pair is None else pair[1, :, cols])
            score = dot_nt(query, key) * (scale * LOG2E)
            if pair is not None:
                valid = (seq + offset >= 0) & (seq + offset < blocks)
                score = jnp.where(valid, score, -1e30)
            scores.append(score)
        top = scores[0]
        for score in scores[1:]:
            top = jnp.maximum(top, score)
        top = jnp.max(top, axis=1, keepdims=True)
        total = jnp.zeros((rows, rows), F32)
        mixed = jnp.zeros((rows, HEAD_DIM), F32)
        for score, value in zip(scores, values):
            weight = jnp.exp2(score - top)
            total = total + weight
            mixed = mixed + dot(weight.astype(BF16), value)
        total = jnp.sum(total, axis=1, keepdims=True)
        att_ref[:, cols] = (mixed / total).astype(BF16)
        lse_all = jnp.where(lane == head, top + jnp.log2(total), lse_all)
    lse_ref[...] = lse_all
    pack_ref[rows:, :rows] = stat_rows(lse_all, heads)
    pack_ref[rows:, rows:] = jnp.zeros((STAT_ROWS, width - rows), BF16)


def out_kernel(att_ref, weight_ref, own_ref, other_ref):
    rows, width = own_ref.shape
    for start in range(0, width, OUT_STEP):
        product = dot(att_ref[...], weight_ref[:, start : start + OUT_STEP]).astype(BF16)
        own_ref[:, start : start + OUT_STEP] = product[:rows]
        other_ref[:, start : start + OUT_STEP] = product[rows:]


def lane_sums(values):
    total = values[:, :HEAD_DIM]
    for start in range(HEAD_DIM, values.shape[1], HEAD_DIM):
        total = total + values[:, start : start + HEAD_DIM]
    return total


def norm_kernel(near_ref, far_ref, residual_ref, gain_ref, unit_ref, sigma_ref, normed_ref):
    rows, width = residual_ref.shape
    spans = [slice(at, at + NORM_STEP) for at in range(0, width, NORM_STEP)]
    total = jnp.zeros((rows, HEAD_DIM), F32)
    for cols in spans:
        stream = residual_ref[:, cols].astype(F32) + near_ref[:, cols].astype(F32) + far_ref[:, cols].astype(F32)
        unit_ref[:, cols] = stream
        total = total + lane_sums(stream)
    mean = jnp.sum(total, axis=-1, keepdims=True) / width
    total = jnp.zeros((rows, HEAD_DIM), F32)
    for cols in spans:
        centered = unit_ref[:, cols] - mean
        total = total + lane_sums(centered * centered)
    sigma = jnp.sqrt(jnp.sum(total, axis=-1, keepdims=True) / width + EPSILON)
    sigma_ref[...] = jnp.broadcast_to(sigma, sigma_ref.shape)
    inverse = 1.0 / sigma
    for cols in spans:
        unit = (unit_ref[:, cols] - mean) * inverse
        unit_ref[:, cols] = unit
        normed_ref[:, cols] = (unit * gain_ref[:, cols]).astype(BF16)


def norm_back_kernel(near_ref, far_ref, cot_ref, gain_ref, unit_ref, sigma_ref, low_ref, scaled_ref):
    rows, width = cot_ref.shape
    spans = [slice(at, at + NORM_STEP) for at in range(0, width, NORM_STEP)]
    total = jnp.zeros((rows, HEAD_DIM), F32)
    total_along = jnp.zeros((rows, HEAD_DIM), F32)
    for cols in spans:
        grad = cot_ref[:, cols].astype(F32) + near_ref[:, cols].astype(F32) + far_ref[:, cols].astype(F32)
        scaled = grad * gain_ref[:, cols]
        scaled_ref[:, cols] = scaled
        total = total + lane_sums(scaled)
        total_along = total_along + lane_sums(scaled * unit_ref[:, cols])
    mean = jnp.sum(total, axis=-1, keepdims=True) / width
    along = jnp.sum(total_along, axis=-1, keepdims=True) / width
    inverse = 1.0 / sigma_ref[:, :1]
    for cols in spans:
        grad = (scaled_ref[:, cols] - mean - unit_ref[:, cols] * along) * inverse
        low_ref[:, cols] = grad.astype(BF16)


def gelu_and_slope(v):
    root = math.sqrt(2.0 / math.pi)
    square = v * v
    t = jnp.tanh(v * (root + root * 0.044715 * square))
    plus = 0.5 + 0.5 * t
    slope = plus + 0.5 * v * (1.0 - t * t) * (root + 3.0 * root * 0.044715 * square)
    return v * plus, slope


def ffn_kernel(
    own_ref, near_ref, up_ref, pick_ref, grad_ref, grad_copy_ref, inverse_ref, gain_ref, merged_ref, hidden_grad_ref
):
    rows = jnp.concatenate([own_ref[...], near_ref[...]], axis=0)
    source = dot(rows, up_ref[...])
    high = source.astype(BF16)
    low = (source - high.astype(F32)).astype(BF16)
    copied = (dot(high, pick_ref[...]) + dot(low, pick_ref[...])) * gain_ref[...]
    act_copy, slope_copy = gelu_and_slope(copied)
    act, slope = gelu_and_slope(source)
    back_copy = (grad_copy_ref[...] * slope_copy).astype(BF16)
    hidden_grad_ref[...] = (grad_ref[...] * slope + dot_nt(back_copy, pick_ref[...])).astype(BF16)
    merged = act + dot_nt(act_copy.astype(BF16), pick_ref[...])
    merged_ref[...] = (merged * inverse_ref[...]).astype(BF16)


def back_kernel(hidden_grad_ref, up_ref, own_ref, other_ref):
    rows, width = own_ref.shape
    for start in range(0, width, OUT_STEP):
        product = dot_nt(hidden_grad_ref[...], up_ref[start : start + OUT_STEP]).astype(BF16)
        own_ref[:, start : start + OUT_STEP] = product[:rows]
        other_ref[:, start : start + OUT_STEP] = product[rows:]


def grad_attended_kernel(own_ref, near_ref, weight_ref, att_ref, pack_ref, delta_ref):
    rows, width = att_ref.shape
    heads = width // HEAD_DIM
    low = jnp.concatenate([own_ref[...], near_ref[...]], axis=0)
    pack_ref[:rows] = dot_nt(low, weight_ref[...]).astype(BF16)
    product = pack_ref[:rows].astype(F32) * att_ref[...].astype(F32)
    lane = lax.broadcasted_iota(jnp.int32, (rows, HEAD_DIM), 1)
    delta = jnp.zeros((rows, HEAD_DIM), F32)
    for head in range(heads):
        part = jnp.sum(product[:, head * HEAD_DIM : (head + 1) * HEAD_DIM], axis=1, keepdims=True)
        delta = jnp.where(lane == head, part, delta)
    delta_ref[...] = delta
    pack_ref[rows:, :rows] = stat_rows(delta, heads)
    pack_ref[rows:, rows:] = jnp.zeros((STAT_ROWS, width - rows), BF16)


def grad_query_kernel(
    scale, place, q_pack, do_pack, lse_ref, delta_ref, k0, v0, kv_a, kv_b, kv_c, kv_d, grad_ref
):
    rows, width = grad_ref.shape
    heads = width // HEAD_DIM
    slab = rows // 4
    seq, blocks, core = place[0], place[1], place[2]
    for head in range(heads):
        cols = slice(head * HEAD_DIM, (head + 1) * HEAD_DIM)
        query, out_grad = q_pack[:rows, cols], do_pack[:rows, cols]
        lse, delta = lse_ref[:, head : head + 1], delta_ref[:, head : head + 1]
        total = jnp.zeros((rows, HEAD_DIM), F32)
        for offset, pair in zip((0,) + nearby_offsets(seq), (None, kv_a, kv_b, kv_c, kv_d)):
            key = k0[:, cols] if pair is None else pair[0, :, cols]
            value = v0[:, cols] if pair is None else pair[1, :, cols]
            score = dot_nt(query, key) * (scale * LOG2E) - lse
            if pair is not None:
                valid = (seq + offset >= 0) & (seq + offset < blocks)
                score = jnp.where(valid, score, -1e30)
            grad_score = jnp.exp2(score) * (dot_nt(out_grad, value) - delta)
            total = total + dot(grad_score.astype(BF16), key)
        total = total * scale
        for index, start in enumerate(local_starts(core, rows)):
            grad_ref[pl.ds(start, slab), cols] = total[index * slab : (index + 1) * slab]


def grad_key_value_kernel(scale, count, start, *refs):
    packs, refs = refs[: 2 * count], refs[2 * count :]
    k0, v0 = refs[:2]
    grad_key_ref, grad_value_ref = refs[-2:]
    rows, width = k0.shape
    heads = width // HEAD_DIM
    for head in range(heads):
        cols = slice(head * HEAD_DIM, (head + 1) * HEAD_DIM)
        key, value = k0[:, cols], v0[:, cols]
        grad_key = jnp.zeros((rows, HEAD_DIM), F32)
        grad_value = jnp.zeros((rows, HEAD_DIM), F32)
        for index in range(count):
            q_pack, do_pack = packs[2 * index], packs[2 * index + 1]
            query, out_grad = q_pack[:rows, cols], do_pack[:rows, cols]
            score = dot_nt(key, query) * (scale * LOG2E) - read_stat(q_pack, head, heads, rows)
            weight = jnp.exp2(score)
            grad_value = grad_value + dot(weight.astype(BF16), out_grad)
            grad_score = weight * (dot_nt(value, out_grad) - read_stat(do_pack, head, heads, rows))
            grad_key = grad_key + dot(grad_score.astype(BF16), query)
        grad_key = grad_key * scale
        if not start:
            grad_key = grad_key + refs[2][:, cols]
            grad_value = grad_value + refs[3][:, cols]
        grad_key_ref[:, cols] = grad_key
        grad_value_ref[:, cols] = grad_value


def shards(
    query_heads,
    key_heads,
    value_heads,
    residual,
    out_weight,
    ln_gain,
    up_source,
    down_source,
    copy_gain,
    neuron_source,
    cotangent,
):
    rows, head_width = query_heads.shape
    model_width = residual.shape[1]
    src_width = up_source.shape[1]
    half = rows // 2
    scale = 1.0 / math.sqrt(HEAD_DIM)
    seq = lax.axis_index("seq")
    blocks = lax.axis_size("seq")
    tp_place = lax.axis_index("tp")
    core, chip = tp_place % 2, tp_place // 2
    place = jnp.stack([seq, jnp.full_like(seq, blocks), core]).astype(jnp.int32)

    kv = jnp.stack([key_heads, value_heads])
    kv_a, kv_b = swap_block(kv, 0), swap_block(kv, 1)

    def half_rows(array, place):
        split = array.reshape(2, 2, half // 2, array.shape[1])
        return lax.dynamic_slice_in_dim(split, place, 1, 1).reshape(half, array.shape[1])

    cot_own = half_rows(cotangent, core)
    cot_local = jnp.concatenate([cot_own, half_rows(cotangent, 1 - core)], axis=0)
    grad_merged = dot_nt(cot_local, down_source)
    kv_a, kv_b, grad_merged = lax.optimization_barrier((kv_a, kv_b, grad_merged))
    kv_c, kv_d = swap_block(kv_b, 0), swap_block(kv_a, 1)

    residual_own = half_rows(residual, core)
    local_source = neuron_source - tp_place * src_width
    pick = (lax.broadcasted_iota(jnp.int32, (src_width, src_width), 0) == local_source[None, :])
    counts = 1.0 + jnp.sum(pick.astype(F32), axis=1)
    pick = pick.astype(BF16)
    inverse = 1.0 / counts
    grad_merged = grad_merged * inverse
    grad_high = grad_merged.astype(BF16)
    grad_rest = (grad_merged - grad_high.astype(F32)).astype(BF16)
    grad_copy = (dot(grad_high, pick) + dot(grad_rest, pick)) * copy_gain
    gain_row = ln_gain.reshape(1, model_width)
    inverse_row = inverse.reshape(1, src_width)
    copy_row = copy_gain.reshape(1, src_width)
    kv_c, kv_d, pick, grad_merged, grad_copy, residual_own = lax.optimization_barrier(
        (kv_c, kv_d, pick, grad_merged, grad_copy, residual_own)
    )
    window = (key_heads, value_heads, kv_a, kv_b, kv_c, kv_d)

    attended, q_pack, lse = call(
        functools.partial(attention_kernel, scale),
        (
            shape((rows, head_width), BF16),
            shape((rows + STAT_ROWS, head_width), BF16),
            shape((rows, HEAD_DIM), F32),
        ),
        [SMEM] + [VMEM] * 7,
    )(place, query_heads, *window)

    def chip_sum(kernel, operands):
        own, other = call(kernel, (shape((half, model_width), BF16),) * 2, [VMEM, VMEM])(*operands)
        near = (own.astype(F32) + swap_core(other).astype(F32)).astype(BF16)
        return near, swap_chip(near)

    near, far = chip_sum(out_kernel, (attended, out_weight))

    q_early = after(q_pack, near)
    far, q_a, q_b = lax.optimization_barrier((far, swap_block(q_early, 0), swap_block(q_early, 1)))

    unit, sigma, normed = call(
        norm_kernel,
        (
            shape((half, model_width), F32),
            shape((half, HEAD_DIM), F32),
            shape((half, model_width), BF16),
        ),
        [VMEM] * 4,
    )(near, far, residual_own, gain_row)
    near_normed = swap_core(normed)
    merged, hidden_grad = call(ffn_kernel, (shape((rows, src_width), BF16),) * 2, [VMEM] * 8)(
        normed, near_normed, up_source, pick, grad_merged, grad_copy, inverse_row, copy_row
    )
    near, far = chip_sum(back_kernel, (hidden_grad, up_source))
    ffn_part = dot(merged, down_source).astype(BF16)
    q_c, q_d = after((q_b, q_a), near)
    q_c, q_d = swap_block(q_c, 0), swap_block(q_d, 1)
    far, ffn_part, q_c, q_d = lax.optimization_barrier((far, ffn_part, q_c, q_d))

    low = call(
        norm_back_kernel,
        shape((half, model_width), BF16),
        [VMEM] * 6,
        scratch=[pltpu.VMEM((half, model_width), F32)],
    )(near, far, cot_own, gain_row, unit, sigma)
    ffn_part = after(ffn_part, low)
    near_low, ffn_near = lax.optimization_barrier((swap_core(low), swap_core(ffn_part[half:])))
    do_pack, delta = call(
        grad_attended_kernel,
        (shape((rows + STAT_ROWS, head_width), BF16), shape((rows, HEAD_DIM), F32)),
        [VMEM] * 4,
    )(low, near_low, out_weight, attended)

    do_a, do_b = swap_block(do_pack, 0), swap_block(do_pack, 1)

    ffn_part = after(ffn_part, do_pack)
    ffn_chip = (ffn_part[:half].astype(F32) + ffn_near.astype(F32)).reshape(2, half // 2, model_width)
    ffn_far = swap_chip(jnp.where(chip == 0, ffn_chip[1], ffn_chip[0]).astype(BF16))
    ffn_mine = jnp.where(chip == 0, ffn_chip[0], ffn_chip[1])

    do_a, do_b, do_own = lax.optimization_barrier((do_a, do_b, do_pack))
    do_c, do_d = swap_block(do_b, 0), swap_block(do_a, 1)
    grad_query = call(
        functools.partial(grad_query_kernel, scale),
        shape((rows, head_width), F32),
        [SMEM] + [VMEM] * 10,
    )(place, q_pack, do_own, lse, delta, *window)

    def grad_key_value(pairs, sums):
        return call(
            functools.partial(grad_key_value_kernel, scale, len(pairs), not sums),
            (shape((rows, head_width), F32),) * 2,
            [VMEM] * (2 * len(pairs) + 2 + len(sums)),
        )(*[pack for pair in pairs for pack in pair], key_heads, value_heads, *sums)

    sums = grad_key_value([(q_pack, do_own), (q_a, do_a), (q_b, do_b)], ())
    own_unit = lax.dynamic_slice_in_dim(unit, chip * (half // 2), half // 2, 0)
    encoded = own_unit * ln_gain + (ffn_mine + ffn_far.astype(F32))
    grad_key, grad_value = grad_key_value([(q_c, do_c), (q_d, do_d)], sums)

    col_width = model_width // lax.axis_size("tp")
    first = jnp.where(core == 0, low, near_low).reshape(2, half // 2, model_width)
    second = jnp.where(core == 0, near_low, low).reshape(2, half // 2, model_width)
    low_all = jnp.stack([first, second], axis=1).reshape(rows, model_width)
    grad_residual = lax.dynamic_slice_in_dim(low_all, tp_place * col_width, col_width, 1).astype(F32)
    return (encoded, grad_query, grad_key, grad_value, grad_residual)


def solution(mesh):
    in_specs = (
        P("seq", "tp"),
        P("seq", "tp"),
        P("seq", "tp"),
        P("seq", None),
        P("tp", None),
        P(),
        P(None, "tp"),
        P("tp", None),
        P("tp"),
        P("tp"),
        P("seq", None),
    )
    out_specs = (
        P(("seq", "tp"), None),
        P("seq", "tp"),
        P("seq", "tp"),
        P("seq", "tp"),
        P("seq", "tp"),
    )
    return jax.shard_map(shards, mesh=mesh, in_specs=in_specs, out_specs=out_specs, check_vma=False)
```

```python
import functools
import math

import jax
import jax.numpy as jnp
from jax import lax
from jax.experimental import pallas as pl
from jax.experimental.pallas import tpu as pltpu
from jax.sharding import PartitionSpec as P

HEAD_DIM = 128
EPSILON = 1e-05
LOG2E = math.log2(math.e)
F32 = jnp.float32
BF16 = jnp.bfloat16
NT = (((1,), (1,)), ((), ()))
STAT_ROWS = 16
VMEM_LIMIT = 16 * 1024 * 1024
OUT_STEP = 512
NORM_STEP = 512
COST = 1024

VMEM = pl.BlockSpec(memory_space=pltpu.VMEM)
SMEM = pl.BlockSpec(memory_space=pltpu.SMEM)


def call(kernel, out_shape, in_specs, scratch=()):
    return pl.pallas_call(
        kernel,
        out_shape=out_shape,
        in_specs=in_specs,
        out_specs=jax.tree.map(lambda _: VMEM, out_shape),
        scratch_shapes=list(scratch),
        compiler_params=pltpu.CompilerParams(vmem_limit_bytes=VMEM_LIMIT),
        cost_estimate=pl.CostEstimate(flops=COST, bytes_accessed=COST, transcendentals=0),
    )


def shape(dims, dtype):
    return jax.ShapeDtypeStruct(dims, dtype)


def dot(a, b):
    return jnp.dot(a, b, preferred_element_type=F32)


def dot_nt(a, b):
    return lax.dot_general(a, b, NT, preferred_element_type=F32)


def swap_core(array):
    return lax.ppermute(array, "tp", [(0, 1), (1, 0), (2, 3), (3, 2)])


def swap_chip(array):
    return lax.ppermute(array, "tp", [(0, 2), (2, 0), (1, 3), (3, 1)])


def after(value, *earlier):
    return lax.optimization_barrier((value, earlier))[0]


def swap_block(array, first):
    count = lax.axis_size("seq")
    ahead = [(i, i + 1) for i in range(first, count - 1, 2)]
    return lax.ppermute(array, "seq", ahead + [(j, i) for i, j in ahead])


def nearby_offsets(seq):
    side = 1 - 2 * (seq % 2)
    return side, -side, 2 * side, -2 * side


def three_parts(values):
    high = values.astype(BF16).astype(F32)
    middle = (values - high).astype(BF16).astype(F32)
    low = values - high - middle
    return high, middle, low


def stat_rows(columns, heads):
    rows = columns.T[:heads]
    parts = three_parts(rows)
    fill = jnp.zeros((STAT_ROWS - 3 * heads, rows.shape[1]), F32)
    return jnp.concatenate(parts + (fill,), axis=0).astype(BF16)


def read_stat(pack, head, heads, rows):
    block = pack[rows : rows + STAT_ROWS, :rows].astype(F32)
    total = block[head : head + 1]
    for part in (1, 2):
        total = total + block[part * heads + head : part * heads + head + 1]
    return total


def local_starts(core, rows):
    slab = rows // 4
    return [(2 * part + (core if own else 1 - core)) * slab for own in (True, False) for part in range(2)]


def attention_kernel(scale, place, q_ref, k0, v0, kv_a, kv_b, kv_c, kv_d, att_ref, pack_ref, lse_ref):
    rows, width = q_ref.shape
    heads = width // HEAD_DIM
    slab = rows // 4
    seq, blocks, core = place[0], place[1], place[2]
    for index, start in enumerate(local_starts(core, rows)):
        pack_ref[index * slab : (index + 1) * slab] = q_ref[pl.ds(start, slab)]
    lane = lax.broadcasted_iota(jnp.int32, (rows, HEAD_DIM), 1)
    lse_all = jnp.zeros((rows, HEAD_DIM), F32)
    for head in range(heads):
        cols = slice(head * HEAD_DIM, (head + 1) * HEAD_DIM)
        query = pack_ref[:rows, cols]
        scores = []
        values = []
        for offset, pair in zip((0,) + nearby_offsets(seq), (None, kv_a, kv_b, kv_c, kv_d)):
            key = k0[:, cols] if pair is None else pair[0, :, cols]
            values.append(v0[:, cols] if pair is None else pair[1, :, cols])
            score = dot_nt(query, key) * (scale * LOG2E)
            if pair is not None:
                valid = (seq + offset >= 0) & (seq + offset < blocks)
                score = jnp.where(valid, score, -1e30)
            scores.append(score)
        top = scores[0]
        for score in scores[1:]:
            top = jnp.maximum(top, score)
        top = jnp.max(top, axis=1, keepdims=True)
        total = jnp.zeros((rows, rows), F32)
        mixed = jnp.zeros((rows, HEAD_DIM), F32)
        for score, value in zip(scores, values):
            weight = jnp.exp2(score - top)
            total = total + weight
            mixed = mixed + dot(weight.astype(BF16), value)
        total = jnp.sum(total, axis=1, keepdims=True)
        att_ref[:, cols] = (mixed / total).astype(BF16)
        lse_all = jnp.where(lane == head, top + jnp.log2(total), lse_all)
    lse_ref[...] = lse_all
    pack_ref[rows:, :rows] = stat_rows(lse_all, heads)
    pack_ref[rows:, rows:] = jnp.zeros((STAT_ROWS, width - rows), BF16)


def out_kernel(att_ref, weight_ref, own_ref, other_ref):
    rows, width = own_ref.shape
    for start in range(0, width, OUT_STEP):
        product = dot(att_ref[...], weight_ref[:, start : start + OUT_STEP]).astype(BF16)
        own_ref[:, start : start + OUT_STEP] = product[:rows]
        other_ref[:, start : start + OUT_STEP] = product[rows:]


def lane_sums(values):
    total = values[:, :HEAD_DIM]
    for start in range(HEAD_DIM, values.shape[1], HEAD_DIM):
        total = total + values[:, start : start + HEAD_DIM]
    return total


def norm_kernel(near_ref, far_ref, residual_ref, gain_ref, unit_ref, sigma_ref, normed_ref):
    rows, width = residual_ref.shape
    spans = [slice(at, at + NORM_STEP) for at in range(0, width, NORM_STEP)]
    total = jnp.zeros((rows, HEAD_DIM), F32)
    for cols in spans:
        stream = residual_ref[:, cols].astype(F32) + near_ref[:, cols].astype(F32) + far_ref[:, cols].astype(F32)
        unit_ref[:, cols] = stream
        total = total + lane_sums(stream)
    mean = jnp.sum(total, axis=-1, keepdims=True) / width
    total = jnp.zeros((rows, HEAD_DIM), F32)
    for cols in spans:
        centered = unit_ref[:, cols] - mean
        total = total + lane_sums(centered * centered)
    sigma = jnp.sqrt(jnp.sum(total, axis=-1, keepdims=True) / width + EPSILON)
    sigma_ref[...] = jnp.broadcast_to(sigma, sigma_ref.shape)
    inverse = 1.0 / sigma
    for cols in spans:
        unit = (unit_ref[:, cols] - mean) * inverse
        unit_ref[:, cols] = unit
        normed_ref[:, cols] = (unit * gain_ref[:, cols]).astype(BF16)


def norm_back_kernel(near_ref, far_ref, cot_ref, gain_ref, unit_ref, sigma_ref, low_ref, scaled_ref):
    rows, width = cot_ref.shape
    spans = [slice(at, at + NORM_STEP) for at in range(0, width, NORM_STEP)]
    total = jnp.zeros((rows, HEAD_DIM), F32)
    total_along = jnp.zeros((rows, HEAD_DIM), F32)
    for cols in spans:
        grad = cot_ref[:, cols].astype(F32) + near_ref[:, cols].astype(F32) + far_ref[:, cols].astype(F32)
        scaled = grad * gain_ref[:, cols]
        scaled_ref[:, cols] = scaled
        total = total + lane_sums(scaled)
        total_along = total_along + lane_sums(scaled * unit_ref[:, cols])
    mean = jnp.sum(total, axis=-1, keepdims=True) / width
    along = jnp.sum(total_along, axis=-1, keepdims=True) / width
    inverse = 1.0 / sigma_ref[:, :1]
    for cols in spans:
        grad = (scaled_ref[:, cols] - mean - unit_ref[:, cols] * along) * inverse
        low_ref[:, cols] = grad.astype(BF16)


def gelu_and_slope(v):
    root = math.sqrt(2.0 / math.pi)
    square = v * v
    t = jnp.tanh(v * (root + root * 0.044715 * square))
    plus = 0.5 + 0.5 * t
    slope = plus + 0.5 * v * (1.0 - t * t) * (root + 3.0 * root * 0.044715 * square)
    return v * plus, slope


def ffn_kernel(
    own_ref, near_ref, up_ref, pick_ref, grad_ref, grad_copy_ref, inverse_ref, gain_ref, merged_ref, hidden_grad_ref
):
    rows = jnp.concatenate([own_ref[...], near_ref[...]], axis=0)
    source = dot(rows, up_ref[...])
    high = source.astype(BF16)
    low = (source - high.astype(F32)).astype(BF16)
    copied = (dot(high, pick_ref[...]) + dot(low, pick_ref[...])) * gain_ref[...]
    act_copy, slope_copy = gelu_and_slope(copied)
    act, slope = gelu_and_slope(source)
    back_copy = (grad_copy_ref[...] * slope_copy).astype(BF16)
    hidden_grad_ref[...] = (grad_ref[...] * slope + dot_nt(back_copy, pick_ref[...])).astype(BF16)
    merged = act + dot_nt(act_copy.astype(BF16), pick_ref[...])
    merged_ref[...] = (merged * inverse_ref[...]).astype(BF16)


def back_kernel(hidden_grad_ref, up_ref, own_ref, other_ref):
    rows, width = own_ref.shape
    for start in range(0, width, OUT_STEP):
        product = dot_nt(hidden_grad_ref[...], up_ref[start : start + OUT_STEP]).astype(BF16)
        own_ref[:, start : start + OUT_STEP] = product[:rows]
        other_ref[:, start : start + OUT_STEP] = product[rows:]


def grad_attended_own_kernel(low_ref, weight_ref, grad_ref):
    grad_ref[...] = dot_nt(low_ref[...], weight_ref[...]).astype(BF16)


def grad_attended_kernel(own_ref, near_ref, weight_ref, att_ref, pack_ref, delta_ref):
    rows, width = att_ref.shape
    heads = width // HEAD_DIM
    pack_ref[: rows // 2] = own_ref[...]
    pack_ref[rows // 2 : rows] = dot_nt(near_ref[...], weight_ref[...]).astype(BF16)
    product = pack_ref[:rows].astype(F32) * att_ref[...].astype(F32)
    lane = lax.broadcasted_iota(jnp.int32, (rows, HEAD_DIM), 1)
    delta = jnp.zeros((rows, HEAD_DIM), F32)
    for head in range(heads):
        part = jnp.sum(product[:, head * HEAD_DIM : (head + 1) * HEAD_DIM], axis=1, keepdims=True)
        delta = jnp.where(lane == head, part, delta)
    delta_ref[...] = delta
    pack_ref[rows:, :rows] = stat_rows(delta, heads)
    pack_ref[rows:, rows:] = jnp.zeros((STAT_ROWS, width - rows), BF16)


def grad_query_kernel(
    scale, place, q_pack, do_pack, lse_ref, delta_ref, k0, v0, kv_a, kv_b, kv_c, kv_d, grad_ref
):
    rows, width = grad_ref.shape
    heads = width // HEAD_DIM
    slab = rows // 4
    seq, blocks, core = place[0], place[1], place[2]
    for head in range(heads):
        cols = slice(head * HEAD_DIM, (head + 1) * HEAD_DIM)
        query, out_grad = q_pack[:rows, cols], do_pack[:rows, cols]
        lse, delta = lse_ref[:, head : head + 1], delta_ref[:, head : head + 1]
        total = jnp.zeros((rows, HEAD_DIM), F32)
        for offset, pair in zip((0,) + nearby_offsets(seq), (None, kv_a, kv_b, kv_c, kv_d)):
            key = k0[:, cols] if pair is None else pair[0, :, cols]
            value = v0[:, cols] if pair is None else pair[1, :, cols]
            score = dot_nt(query, key) * (scale * LOG2E) - lse
            if pair is not None:
                valid = (seq + offset >= 0) & (seq + offset < blocks)
                score = jnp.where(valid, score, -1e30)
            grad_score = jnp.exp2(score) * (dot_nt(out_grad, value) - delta)
            total = total + dot(grad_score.astype(BF16), key)
        total = total * scale
        for index, start in enumerate(local_starts(core, rows)):
            grad_ref[pl.ds(start, slab), cols] = total[index * slab : (index + 1) * slab]


def grad_key_value_kernel(scale, count, start, *refs):
    packs, refs = refs[: 2 * count], refs[2 * count :]
    k0, v0 = refs[:2]
    grad_key_ref, grad_value_ref = refs[-2:]
    rows, width = k0.shape
    heads = width // HEAD_DIM
    for head in range(heads):
        cols = slice(head * HEAD_DIM, (head + 1) * HEAD_DIM)
        key, value = k0[:, cols], v0[:, cols]
        grad_key = jnp.zeros((rows, HEAD_DIM), F32)
        grad_value = jnp.zeros((rows, HEAD_DIM), F32)
        for index in range(count):
            q_pack, do_pack = packs[2 * index], packs[2 * index + 1]
            query, out_grad = q_pack[:rows, cols], do_pack[:rows, cols]
            score = dot_nt(key, query) * (scale * LOG2E) - read_stat(q_pack, head, heads, rows)
            weight = jnp.exp2(score)
            grad_value = grad_value + dot(weight.astype(BF16), out_grad)
            grad_score = weight * (dot_nt(value, out_grad) - read_stat(do_pack, head, heads, rows))
            grad_key = grad_key + dot(grad_score.astype(BF16), query)
        grad_key = grad_key * scale
        if not start:
            grad_key = grad_key + refs[2][:, cols]
            grad_value = grad_value + refs[3][:, cols]
        grad_key_ref[:, cols] = grad_key
        grad_value_ref[:, cols] = grad_value


def shards(
    query_heads,
    key_heads,
    value_heads,
    residual,
    out_weight,
    ln_gain,
    up_source,
    down_source,
    copy_gain,
    neuron_source,
    cotangent,
):
    rows, head_width = query_heads.shape
    model_width = residual.shape[1]
    src_width = up_source.shape[1]
    half = rows // 2
    scale = 1.0 / math.sqrt(HEAD_DIM)
    seq = lax.axis_index("seq")
    blocks = lax.axis_size("seq")
    tp_place = lax.axis_index("tp")
    core, chip = tp_place % 2, tp_place // 2
    place = jnp.stack([seq, jnp.full_like(seq, blocks), core]).astype(jnp.int32)

    kv = jnp.stack([key_heads, value_heads])
    kv_a, kv_b = swap_block(kv, 0), swap_block(kv, 1)

    def half_rows(array, place):
        split = array.reshape(2, 2, half // 2, array.shape[1])
        return lax.dynamic_slice_in_dim(split, place, 1, 1).reshape(half, array.shape[1])

    cot_own = half_rows(cotangent, core)
    cot_local = jnp.concatenate([cot_own, half_rows(cotangent, 1 - core)], axis=0)
    grad_merged = dot_nt(cot_local, down_source)
    kv_a, kv_b, grad_merged = lax.optimization_barrier((kv_a, kv_b, grad_merged))
    kv_c, kv_d = swap_block(kv_b, 0), swap_block(kv_a, 1)

    residual_own = half_rows(residual, core)
    local_source = neuron_source - tp_place * src_width
    pick = (lax.broadcasted_iota(jnp.int32, (src_width, src_width), 0) == local_source[None, :])
    counts = 1.0 + jnp.sum(pick.astype(F32), axis=1)
    pick = pick.astype(BF16)
    inverse = 1.0 / counts
    grad_merged = grad_merged * inverse
    grad_high = grad_merged.astype(BF16)
    grad_rest = (grad_merged - grad_high.astype(F32)).astype(BF16)
    grad_copy = (dot(grad_high, pick) + dot(grad_rest, pick)) * copy_gain
    gain_row = ln_gain.reshape(1, model_width)
    inverse_row = inverse.reshape(1, src_width)
    copy_row = copy_gain.reshape(1, src_width)
    kv_c, kv_d, pick, grad_merged, grad_copy, residual_own = lax.optimization_barrier(
        (kv_c, kv_d, pick, grad_merged, grad_copy, residual_own)
    )
    window = (key_heads, value_heads, kv_a, kv_b, kv_c, kv_d)

    attended, q_pack, lse = call(
        functools.partial(attention_kernel, scale),
        (
            shape((rows, head_width), BF16),
            shape((rows + STAT_ROWS, head_width), BF16),
            shape((rows, HEAD_DIM), F32),
        ),
        [SMEM] + [VMEM] * 7,
    )(place, query_heads, *window)

    def two_parts(kernel, operands):
        return call(kernel, (shape((half, model_width), BF16),) * 2, [VMEM, VMEM])(*operands)

    def chip_sum(own, other):
        return own.astype(F32) + swap_core(other).astype(F32)

    near = chip_sum(*two_parts(out_kernel, (attended, out_weight))).astype(BF16)
    far = swap_chip(near)

    far, q_a = lax.optimization_barrier((far, swap_block(after(q_pack, near), 0)))

    unit, sigma, normed = call(
        norm_kernel,
        (
            shape((half, model_width), F32),
            shape((half, HEAD_DIM), F32),
            shape((half, model_width), BF16),
        ),
        [VMEM] * 4,
    )(near, far, residual_own, gain_row)
    near_normed = swap_core(normed)
    merged, hidden_grad = call(ffn_kernel, (shape((rows, src_width), BF16),) * 2, [VMEM] * 8)(
        normed, near_normed, up_source, pick, grad_merged, grad_copy, inverse_row, copy_row
    )
    ffn_parts = two_parts(out_kernel, (merged, down_source))
    hidden_grad, ffn_parts, q_b = lax.optimization_barrier(
        (hidden_grad, ffn_parts, swap_block(after(q_pack, normed), 1))
    )
    near = chip_sum(*two_parts(back_kernel, (hidden_grad, up_source))).astype(BF16)
    far = swap_chip(near)
    ffn_chip = chip_sum(*ffn_parts).reshape(2, half // 2, model_width)
    ffn_send = jnp.where(chip == 0, ffn_chip[1], ffn_chip[0]).astype(BF16)
    ffn_mine = jnp.where(chip == 0, ffn_chip[0], ffn_chip[1])
    q_c = swap_block(after(q_b, near), 0)
    far, ffn_send, ffn_mine, q_c = lax.optimization_barrier((far, ffn_send, ffn_mine, q_c))

    low = call(
        norm_back_kernel,
        shape((half, model_width), BF16),
        [VMEM] * 6,
        scratch=[pltpu.VMEM((half, model_width), F32)],
    )(near, far, cot_own, gain_row, unit, sigma)
    near_low = swap_core(low)
    ffn_far = swap_chip(after(ffn_send, low))
    grad_own = call(grad_attended_own_kernel, shape((half, head_width), BF16), [VMEM] * 2)(low, out_weight)
    near_low, grad_own = lax.optimization_barrier((near_low, grad_own))
    do_pack, delta = call(
        grad_attended_kernel,
        (shape((rows + STAT_ROWS, head_width), BF16), shape((rows, HEAD_DIM), F32)),
        [VMEM] * 4,
    )(grad_own, near_low, out_weight, attended)

    do_a, do_b = swap_block(do_pack, 0), swap_block(do_pack, 1)

    q_d = swap_block(after(q_a, do_pack), 1)
    do_a, do_b, do_own = lax.optimization_barrier((do_a, do_b, do_pack))
    do_c, do_d = swap_block(do_b, 0), swap_block(do_a, 1)
    grad_query = call(
        functools.partial(grad_query_kernel, scale),
        shape((rows, head_width), F32),
        [SMEM] + [VMEM] * 10,
    )(place, q_pack, do_own, lse, delta, *window)

    def grad_key_value(pairs, sums):
        return call(
            functools.partial(grad_key_value_kernel, scale, len(pairs), not sums),
            (shape((rows, head_width), F32),) * 2,
            [VMEM] * (2 * len(pairs) + 2 + len(sums)),
        )(*[pack for pair in pairs for pack in pair], key_heads, value_heads, *sums)

    sums = grad_key_value([(q_pack, do_own), (q_a, do_a), (q_b, do_b)], ())
    own_unit = lax.dynamic_slice_in_dim(unit, chip * (half // 2), half // 2, 0)
    encoded = own_unit * ln_gain + (ffn_mine + after(ffn_far, grad_query, *sums).astype(F32))
    grad_key, grad_value = grad_key_value([(q_c, do_c), (q_d, do_d)], sums)

    col_width = model_width // lax.axis_size("tp")
    first = jnp.where(core == 0, low, near_low).reshape(2, half // 2, model_width)
    second = jnp.where(core == 0, near_low, low).reshape(2, half // 2, model_width)
    low_all = jnp.stack([first, second], axis=1).reshape(rows, model_width)
    grad_residual = lax.dynamic_slice_in_dim(low_all, tp_place * col_width, col_width, 1).astype(F32)
    return (encoded, grad_query, grad_key, grad_value, grad_residual)


def solution(mesh):
    in_specs = (
        P("seq", "tp"),
        P("seq", "tp"),
        P("seq", "tp"),
        P("seq", None),
        P("tp", None),
        P(),
        P(None, "tp"),
        P("tp", None),
        P("tp"),
        P("tp"),
        P("seq", None),
    )
    out_specs = (
        P(("seq", "tp"), None),
        P("seq", "tp"),
        P("seq", "tp"),
        P("seq", "tp"),
        P("seq", "tp"),
    )
    return jax.shard_map(shards, mesh=mesh, in_specs=in_specs, out_specs=out_specs, check_vma=False)
```

```python
import functools
import math

import jax
import jax.numpy as jnp
from jax import lax
from jax.experimental import pallas as pl
from jax.experimental.pallas import tpu as pltpu
from jax.sharding import PartitionSpec as P

HEAD_DIM = 128
EPSILON = 1e-05
LOG2E = math.log2(math.e)
F32 = jnp.float32
BF16 = jnp.bfloat16
NT = (((1,), (1,)), ((), ()))
STAT_ROWS = 16
VMEM_LIMIT = 16 * 1024 * 1024
OUT_STEP = 512
NORM_STEP = 512
COST = 1024

VMEM = pl.BlockSpec(memory_space=pltpu.VMEM)
SMEM = pl.BlockSpec(memory_space=pltpu.SMEM)


def call(kernel, out_shape, in_specs, scratch=()):
    return pl.pallas_call(
        kernel,
        out_shape=out_shape,
        in_specs=in_specs,
        out_specs=jax.tree.map(lambda _: VMEM, out_shape),
        scratch_shapes=list(scratch),
        compiler_params=pltpu.CompilerParams(vmem_limit_bytes=VMEM_LIMIT),
        cost_estimate=pl.CostEstimate(flops=COST, bytes_accessed=COST, transcendentals=0),
    )


def shape(dims, dtype):
    return jax.ShapeDtypeStruct(dims, dtype)


def dot(a, b):
    return jnp.dot(a, b, preferred_element_type=F32)


def dot_nt(a, b):
    return lax.dot_general(a, b, NT, preferred_element_type=F32)


def swap_core(array):
    return lax.ppermute(array, "tp", [(0, 1), (1, 0), (2, 3), (3, 2)])


def swap_chip(array):
    return lax.ppermute(array, "tp", [(0, 2), (2, 0), (1, 3), (3, 1)])


def after(value, *earlier):
    return lax.optimization_barrier((value, earlier))[0]


def swap_block(array, first):
    count = lax.axis_size("seq")
    ahead = [(i, i + 1) for i in range(first, count - 1, 2)]
    return lax.ppermute(array, "seq", ahead + [(j, i) for i, j in ahead])


def nearby_offsets(seq):
    side = 1 - 2 * (seq % 2)
    return side, -side, 2 * side, -2 * side


def three_parts(values):
    high = values.astype(BF16).astype(F32)
    middle = (values - high).astype(BF16).astype(F32)
    low = values - high - middle
    return high, middle, low


def stat_rows(columns, heads):
    rows = columns.T[:heads]
    parts = three_parts(rows)
    fill = jnp.zeros((STAT_ROWS - 3 * heads, rows.shape[1]), F32)
    return jnp.concatenate(parts + (fill,), axis=0).astype(BF16)


def read_stat(pack, head, heads, rows):
    block = pack[rows : rows + STAT_ROWS, :rows].astype(F32)
    total = block[head : head + 1]
    for part in (1, 2):
        total = total + block[part * heads + head : part * heads + head + 1]
    return total


def local_starts(core, rows):
    slab = rows // 4
    return [(2 * part + (core if own else 1 - core)) * slab for own in (True, False) for part in range(2)]


def attention_kernel(scale, place, q_ref, *refs):
    key_refs, value_refs = refs[0:10:2], refs[1:10:2]
    att_ref, pack_ref, lse_ref = refs[10:]
    rows, width = q_ref.shape
    heads = width // HEAD_DIM
    slab = rows // 4
    seq, blocks, core = place[0], place[1], place[2]
    for index, start in enumerate(local_starts(core, rows)):
        pack_ref[index * slab : (index + 1) * slab] = q_ref[pl.ds(start, slab)]
    lane = lax.broadcasted_iota(jnp.int32, (rows, HEAD_DIM), 1)
    lse_all = jnp.zeros((rows, HEAD_DIM), F32)
    for head in range(heads):
        cols = slice(head * HEAD_DIM, (head + 1) * HEAD_DIM)
        query = pack_ref[:rows, cols]
        scores = []
        values = []
        for index, offset in enumerate((0,) + nearby_offsets(seq)):
            values.append(value_refs[index][:, cols])
            score = dot_nt(query, key_refs[index][:, cols]) * (scale * LOG2E)
            if index > 0:
                valid = (seq + offset >= 0) & (seq + offset < blocks)
                score = jnp.where(valid, score, -1e30)
            scores.append(score)
        top = scores[0]
        for score in scores[1:]:
            top = jnp.maximum(top, score)
        top = jnp.max(top, axis=1, keepdims=True)
        total = jnp.zeros((rows, rows), F32)
        mixed = jnp.zeros((rows, HEAD_DIM), F32)
        for score, value in zip(scores, values):
            weight = jnp.exp2(score - top)
            total = total + weight
            mixed = mixed + dot(weight.astype(BF16), value)
        total = jnp.sum(total, axis=1, keepdims=True)
        att_ref[:, cols] = (mixed / total).astype(BF16)
        lse_all = jnp.where(lane == head, top + jnp.log2(total), lse_all)
    lse_ref[...] = lse_all
    pack_ref[rows:, :rows] = stat_rows(lse_all, heads)
    pack_ref[rows:, rows:] = jnp.zeros((STAT_ROWS, width - rows), BF16)


def out_kernel(att_ref, weight_ref, own_ref, other_ref):
    rows, width = own_ref.shape
    for start in range(0, width, OUT_STEP):
        product = dot(att_ref[...], weight_ref[:, start : start + OUT_STEP]).astype(BF16)
        own_ref[:, start : start + OUT_STEP] = product[:rows]
        other_ref[:, start : start + OUT_STEP] = product[rows:]


def lane_sums(values):
    total = values[:, :HEAD_DIM]
    for start in range(HEAD_DIM, values.shape[1], HEAD_DIM):
        total = total + values[:, start : start + HEAD_DIM]
    return total


def norm_kernel(near_ref, far_ref, residual_ref, gain_ref, unit_ref, sigma_ref, normed_ref):
    rows, width = residual_ref.shape
    spans = [slice(at, at + NORM_STEP) for at in range(0, width, NORM_STEP)]
    total = jnp.zeros((rows, HEAD_DIM), F32)
    for cols in spans:
        stream = residual_ref[:, cols].astype(F32) + near_ref[:, cols].astype(F32) + far_ref[:, cols].astype(F32)
        unit_ref[:, cols] = stream
        total = total + lane_sums(stream)
    mean = jnp.sum(total, axis=-1, keepdims=True) / width
    total = jnp.zeros((rows, HEAD_DIM), F32)
    for cols in spans:
        centered = unit_ref[:, cols] - mean
        total = total + lane_sums(centered * centered)
    sigma = jnp.sqrt(jnp.sum(total, axis=-1, keepdims=True) / width + EPSILON)
    sigma_ref[...] = jnp.broadcast_to(sigma, sigma_ref.shape)
    inverse = 1.0 / sigma
    for cols in spans:
        unit = (unit_ref[:, cols] - mean) * inverse
        unit_ref[:, cols] = unit
        normed_ref[:, cols] = (unit * gain_ref[:, cols]).astype(BF16)


def norm_back_kernel(near_ref, far_ref, cot_ref, gain_ref, unit_ref, sigma_ref, low_ref, scaled_ref):
    rows, width = cot_ref.shape
    spans = [slice(at, at + NORM_STEP) for at in range(0, width, NORM_STEP)]
    total = jnp.zeros((rows, HEAD_DIM), F32)
    total_along = jnp.zeros((rows, HEAD_DIM), F32)
    for cols in spans:
        grad = cot_ref[:, cols].astype(F32) + near_ref[:, cols].astype(F32) + far_ref[:, cols].astype(F32)
        scaled = grad * gain_ref[:, cols]
        scaled_ref[:, cols] = scaled
        total = total + lane_sums(scaled)
        total_along = total_along + lane_sums(scaled * unit_ref[:, cols])
    mean = jnp.sum(total, axis=-1, keepdims=True) / width
    along = jnp.sum(total_along, axis=-1, keepdims=True) / width
    inverse = 1.0 / sigma_ref[:, :1]
    for cols in spans:
        grad = (scaled_ref[:, cols] - mean - unit_ref[:, cols] * along) * inverse
        low_ref[:, cols] = grad.astype(BF16)


def gelu_and_slope(v):
    root = math.sqrt(2.0 / math.pi)
    square = v * v
    t = jnp.tanh(v * (root + root * 0.044715 * square))
    plus = 0.5 + 0.5 * t
    slope = plus + 0.5 * v * (1.0 - t * t) * (root + 3.0 * root * 0.044715 * square)
    return v * plus, slope


def ffn_kernel(
    own_ref, near_ref, up_ref, pick_ref, grad_ref, grad_copy_ref, inverse_ref, gain_ref, merged_ref, hidden_grad_ref
):
    rows = jnp.concatenate([own_ref[...], near_ref[...]], axis=0)
    source = dot(rows, up_ref[...])
    high = source.astype(BF16)
    low = (source - high.astype(F32)).astype(BF16)
    copied = (dot(high, pick_ref[...]) + dot(low, pick_ref[...])) * gain_ref[...]
    act_copy, slope_copy = gelu_and_slope(copied)
    act, slope = gelu_and_slope(source)
    back_copy = (grad_copy_ref[...] * slope_copy).astype(BF16)
    hidden_grad_ref[...] = (grad_ref[...] * slope + dot_nt(back_copy, pick_ref[...])).astype(BF16)
    merged = act + dot_nt(act_copy.astype(BF16), pick_ref[...])
    merged_ref[...] = (merged * inverse_ref[...]).astype(BF16)


def back_kernel(hidden_grad_ref, up_ref, own_ref, other_ref):
    rows, width = own_ref.shape
    for start in range(0, width, OUT_STEP):
        product = dot_nt(hidden_grad_ref[...], up_ref[start : start + OUT_STEP]).astype(BF16)
        own_ref[:, start : start + OUT_STEP] = product[:rows]
        other_ref[:, start : start + OUT_STEP] = product[rows:]


def grad_attended_own_kernel(low_ref, weight_ref, grad_ref):
    grad_ref[...] = dot_nt(low_ref[...], weight_ref[...]).astype(BF16)


def grad_attended_kernel(own_ref, near_ref, weight_ref, att_ref, pack_ref, delta_ref):
    rows, width = att_ref.shape
    heads = width // HEAD_DIM
    pack_ref[: rows // 2] = own_ref[...]
    pack_ref[rows // 2 : rows] = dot_nt(near_ref[...], weight_ref[...]).astype(BF16)
    product = pack_ref[:rows].astype(F32) * att_ref[...].astype(F32)
    lane = lax.broadcasted_iota(jnp.int32, (rows, HEAD_DIM), 1)
    delta = jnp.zeros((rows, HEAD_DIM), F32)
    for head in range(heads):
        part = jnp.sum(product[:, head * HEAD_DIM : (head + 1) * HEAD_DIM], axis=1, keepdims=True)
        delta = jnp.where(lane == head, part, delta)
    delta_ref[...] = delta
    pack_ref[rows:, :rows] = stat_rows(delta, heads)
    pack_ref[rows:, rows:] = jnp.zeros((STAT_ROWS, width - rows), BF16)


def grad_query_kernel(scale, place, q_pack, do_pack, lse_ref, delta_ref, *refs):
    key_refs, value_refs, grad_ref = refs[0:10:2], refs[1:10:2], refs[10]
    rows, width = grad_ref.shape
    heads = width // HEAD_DIM
    slab = rows // 4
    seq, blocks, core = place[0], place[1], place[2]
    for head in range(heads):
        cols = slice(head * HEAD_DIM, (head + 1) * HEAD_DIM)
        query, out_grad = q_pack[:rows, cols], do_pack[:rows, cols]
        lse, delta = lse_ref[:, head : head + 1], delta_ref[:, head : head + 1]
        total = jnp.zeros((rows, HEAD_DIM), F32)
        for index, offset in enumerate((0,) + nearby_offsets(seq)):
            key, value = key_refs[index][:, cols], value_refs[index][:, cols]
            score = dot_nt(query, key) * (scale * LOG2E) - lse
            if index > 0:
                valid = (seq + offset >= 0) & (seq + offset < blocks)
                score = jnp.where(valid, score, -1e30)
            grad_score = jnp.exp2(score) * (dot_nt(out_grad, value) - delta)
            total = total + dot(grad_score.astype(BF16), key)
        total = total * scale
        for index, start in enumerate(local_starts(core, rows)):
            grad_ref[pl.ds(start, slab), cols] = total[index * slab : (index + 1) * slab]


def grad_key_value_kernel(scale, count, start, *refs):
    packs, refs = refs[: 2 * count], refs[2 * count :]
    k0, v0 = refs[:2]
    grad_key_ref, grad_value_ref = refs[-2:]
    rows, width = k0.shape
    heads = width // HEAD_DIM
    for head in range(heads):
        cols = slice(head * HEAD_DIM, (head + 1) * HEAD_DIM)
        key, value = k0[:, cols], v0[:, cols]
        grad_key = jnp.zeros((rows, HEAD_DIM), F32)
        grad_value = jnp.zeros((rows, HEAD_DIM), F32)
        for index in range(count):
            q_pack, do_pack = packs[2 * index], packs[2 * index + 1]
            query, out_grad = q_pack[:rows, cols], do_pack[:rows, cols]
            score = dot_nt(key, query) * (scale * LOG2E) - read_stat(q_pack, head, heads, rows)
            weight = jnp.exp2(score)
            grad_value = grad_value + dot(weight.astype(BF16), out_grad)
            grad_score = weight * (dot_nt(value, out_grad) - read_stat(do_pack, head, heads, rows))
            grad_key = grad_key + dot(grad_score.astype(BF16), query)
        grad_key = grad_key * scale
        if not start:
            grad_key = grad_key + refs[2][:, cols]
            grad_value = grad_value + refs[3][:, cols]
        grad_key_ref[:, cols] = grad_key
        grad_value_ref[:, cols] = grad_value


def shards(
    query_heads,
    key_heads,
    value_heads,
    residual,
    out_weight,
    ln_gain,
    up_source,
    down_source,
    copy_gain,
    neuron_source,
    cotangent,
):
    rows, head_width = query_heads.shape
    model_width = residual.shape[1]
    src_width = up_source.shape[1]
    half = rows // 2
    scale = 1.0 / math.sqrt(HEAD_DIM)
    seq = lax.axis_index("seq")
    blocks = lax.axis_size("seq")
    tp_place = lax.axis_index("tp")
    core, chip = tp_place % 2, tp_place // 2
    place = jnp.stack([seq, jnp.full_like(seq, blocks), core]).astype(jnp.int32)

    window = [key_heads, value_heads]
    first = [(swap_block(array, 0), swap_block(array, 1)) for array in (key_heads, value_heads)]
    second = [(swap_block(b, 0), swap_block(a, 1)) for a, b in first]
    for (keys, values) in zip(first[0] + second[0], first[1] + second[1]):
        window += [keys, values]

    attended, q_pack, lse = call(
        functools.partial(attention_kernel, scale),
        (
            shape((rows, head_width), BF16),
            shape((rows + STAT_ROWS, head_width), BF16),
            shape((rows, HEAD_DIM), F32),
        ),
        [SMEM] + [VMEM] * 11,
    )(place, query_heads, *window)

    def two_parts(kernel, operands):
        return call(kernel, (shape((half, model_width), BF16),) * 2, [VMEM, VMEM])(*operands)

    def chip_sum(own, other):
        return own.astype(F32) + swap_core(other).astype(F32)

    near = chip_sum(*two_parts(out_kernel, (attended, out_weight))).astype(BF16)
    far = swap_chip(near)

    def half_rows(array, place):
        split = array.reshape(2, 2, half // 2, array.shape[1])
        return lax.dynamic_slice_in_dim(split, place, 1, 1).reshape(half, array.shape[1])

    cot_own = half_rows(cotangent, core)
    cot_local = jnp.concatenate([cot_own, half_rows(cotangent, 1 - core)], axis=0)
    grad_merged = dot_nt(after(cot_local, near), down_source)

    residual_own = half_rows(residual, core)
    local_source = neuron_source - tp_place * src_width
    pick = (lax.broadcasted_iota(jnp.int32, (src_width, src_width), 0) == local_source[None, :])
    counts = 1.0 + jnp.sum(pick.astype(F32), axis=1)
    pick = pick.astype(BF16)
    inverse = 1.0 / counts
    grad_merged = grad_merged * inverse
    grad_high = grad_merged.astype(BF16)
    grad_rest = (grad_merged - grad_high.astype(F32)).astype(BF16)
    grad_copy = (dot(grad_high, pick) + dot(grad_rest, pick)) * copy_gain
    gain_row = ln_gain.reshape(1, model_width)
    inverse_row = inverse.reshape(1, src_width)
    copy_row = copy_gain.reshape(1, src_width)

    far, pick, grad_merged, grad_copy = lax.optimization_barrier((far, pick, grad_merged, grad_copy))

    far, q_a = lax.optimization_barrier((far, swap_block(after(q_pack, near), 0)))

    unit, sigma, normed = call(
        norm_kernel,
        (
            shape((half, model_width), F32),
            shape((half, HEAD_DIM), F32),
            shape((half, model_width), BF16),
        ),
        [VMEM] * 4,
    )(near, far, residual_own, gain_row)
    near_normed = swap_core(normed)
    merged, hidden_grad = call(ffn_kernel, (shape((rows, src_width), BF16),) * 2, [VMEM] * 8)(
        normed, near_normed, up_source, pick, grad_merged, grad_copy, inverse_row, copy_row
    )
    ffn_parts = two_parts(out_kernel, (merged, down_source))
    hidden_grad, ffn_parts, q_b = lax.optimization_barrier(
        (hidden_grad, ffn_parts, swap_block(after(q_pack, normed), 1))
    )
    near = chip_sum(*two_parts(back_kernel, (hidden_grad, up_source))).astype(BF16)
    far = swap_chip(near)
    ffn_chip = chip_sum(*ffn_parts).reshape(2, half // 2, model_width)
    ffn_send = jnp.where(chip == 0, ffn_chip[1], ffn_chip[0]).astype(BF16)
    ffn_mine = jnp.where(chip == 0, ffn_chip[0], ffn_chip[1])
    q_c = swap_block(after(q_b, near), 0)
    far, ffn_send, ffn_mine, q_c = lax.optimization_barrier((far, ffn_send, ffn_mine, q_c))

    low = call(
        norm_back_kernel,
        shape((half, model_width), BF16),
        [VMEM] * 6,
        scratch=[pltpu.VMEM((half, model_width), F32)],
    )(near, far, cot_own, gain_row, unit, sigma)
    near_low = swap_core(low)
    ffn_far = swap_chip(after(ffn_send, low))
    grad_own = call(grad_attended_own_kernel, shape((half, head_width), BF16), [VMEM] * 2)(low, out_weight)
    near_low, grad_own = lax.optimization_barrier((near_low, grad_own))
    do_pack, delta = call(
        grad_attended_kernel,
        (shape((rows + STAT_ROWS, head_width), BF16), shape((rows, HEAD_DIM), F32)),
        [VMEM] * 4,
    )(grad_own, near_low, out_weight, attended)

    do_a, do_b = swap_block(do_pack, 0), swap_block(do_pack, 1)

    q_d = swap_block(after(q_a, do_pack), 1)
    do_a, do_b, do_own = lax.optimization_barrier((do_a, do_b, do_pack))
    do_c, do_d = swap_block(do_b, 0), swap_block(do_a, 1)
    grad_query = call(
        functools.partial(grad_query_kernel, scale),
        shape((rows, head_width), F32),
        [SMEM] + [VMEM] * 14,
    )(place, q_pack, do_own, lse, delta, *window)

    def grad_key_value(pairs, sums):
        return call(
            functools.partial(grad_key_value_kernel, scale, len(pairs), not sums),
            (shape((rows, head_width), F32),) * 2,
            [VMEM] * (2 * len(pairs) + 2 + len(sums)),
        )(*[pack for pair in pairs for pack in pair], key_heads, value_heads, *sums)

    sums = grad_key_value([(q_pack, do_own), (q_a, do_a), (q_b, do_b)], ())
    own_unit = lax.dynamic_slice_in_dim(unit, chip * (half // 2), half // 2, 0)
    encoded = own_unit * ln_gain + (ffn_mine + after(ffn_far, grad_query, *sums).astype(F32))
    grad_key, grad_value = grad_key_value([(q_c, do_c), (q_d, do_d)], sums)

    col_width = model_width // lax.axis_size("tp")
    first = jnp.where(core == 0, low, near_low).reshape(2, half // 2, model_width)
    second = jnp.where(core == 0, near_low, low).reshape(2, half // 2, model_width)
    low_all = jnp.stack([first, second], axis=1).reshape(rows, model_width)
    grad_residual = lax.dynamic_slice_in_dim(low_all, tp_place * col_width, col_width, 1).astype(F32)
    return (encoded, grad_query, grad_key, grad_value, grad_residual)


def solution(mesh):
    in_specs = (
        P("seq", "tp"),
        P("seq", "tp"),
        P("seq", "tp"),
        P("seq", None),
        P("tp", None),
        P(),
        P(None, "tp"),
        P("tp", None),
        P("tp"),
        P("tp"),
        P("seq", None),
    )
    out_specs = (
        P(("seq", "tp"), None),
        P("seq", "tp"),
        P("seq", "tp"),
        P("seq", "tp"),
        P("seq", "tp"),
    )
    return jax.shard_map(shards, mesh=mesh, in_specs=in_specs, out_specs=out_specs, check_vma=False)
```

```python
import functools
import math

import jax
import jax.numpy as jnp
from jax import lax
from jax.experimental import pallas as pl
from jax.experimental.pallas import tpu as pltpu
from jax.sharding import PartitionSpec as P

HEAD_DIM = 128
EPSILON = 1e-05
LOG2E = math.log2(math.e)
F32 = jnp.float32
BF16 = jnp.bfloat16
NT = (((1,), (1,)), ((), ()))
STAT_ROWS = 16
VMEM_LIMIT = 16 * 1024 * 1024
OUT_STEP = 512
NORM_STEP = 512
COST = 1024

VMEM = pl.BlockSpec(memory_space=pltpu.VMEM)
SMEM = pl.BlockSpec(memory_space=pltpu.SMEM)


def call(kernel, out_shape, in_specs, scratch=()):
    return pl.pallas_call(
        kernel,
        out_shape=out_shape,
        in_specs=in_specs,
        out_specs=jax.tree.map(lambda _: VMEM, out_shape),
        scratch_shapes=list(scratch),
        compiler_params=pltpu.CompilerParams(vmem_limit_bytes=VMEM_LIMIT),
        cost_estimate=pl.CostEstimate(flops=COST, bytes_accessed=COST, transcendentals=0),
    )


def shape(dims, dtype):
    return jax.ShapeDtypeStruct(dims, dtype)


def dot(a, b):
    return jnp.dot(a, b, preferred_element_type=F32)


def dot_nt(a, b):
    return lax.dot_general(a, b, NT, preferred_element_type=F32)


def swap_core(array):
    return lax.ppermute(array, "tp", [(0, 1), (1, 0), (2, 3), (3, 2)])


def swap_chip(array):
    return lax.ppermute(array, "tp", [(0, 2), (2, 0), (1, 3), (3, 1)])


def after(value, *earlier):
    return lax.optimization_barrier((value, earlier))[0]


def swap_block(array, first):
    count = lax.axis_size("seq")
    ahead = [(i, i + 1) for i in range(first, count - 1, 2)]
    return lax.ppermute(array, "seq", ahead + [(j, i) for i, j in ahead])


def nearby_offsets(seq):
    side = 2 * (seq % 2) - 1
    return side, -side, 2 * side, -2 * side


def three_parts(values):
    high = values.astype(BF16).astype(F32)
    middle = (values - high).astype(BF16).astype(F32)
    low = values - high - middle
    return high, middle, low


def stat_rows(columns, heads):
    rows = columns.T[:heads]
    parts = three_parts(rows)
    fill = jnp.zeros((STAT_ROWS - 3 * heads, rows.shape[1]), F32)
    return jnp.concatenate(parts + (fill,), axis=0).astype(BF16)


def read_stat(pack, head, heads, rows):
    block = pack[rows : rows + STAT_ROWS, :rows].astype(F32)
    total = block[head : head + 1]
    for part in (1, 2):
        total = total + block[part * heads + head : part * heads + head + 1]
    return total


def local_starts(core, rows):
    slab = rows // 4
    return [(2 * part + (core if own else 1 - core)) * slab for own in (True, False) for part in range(2)]


def attention_kernel(scale, place, q_ref, *refs):
    key_refs, value_refs = refs[0:10:2], refs[1:10:2]
    att_ref, pack_ref, lse_ref = refs[10:]
    rows, width = q_ref.shape
    heads = width // HEAD_DIM
    slab = rows // 4
    seq, blocks, core = place[0], place[1], place[2]
    for index, start in enumerate(local_starts(core, rows)):
        pack_ref[index * slab : (index + 1) * slab] = q_ref[pl.ds(start, slab)]
    lane = lax.broadcasted_iota(jnp.int32, (rows, HEAD_DIM), 1)
    lse_all = jnp.zeros((rows, HEAD_DIM), F32)
    for head in range(heads):
        cols = slice(head * HEAD_DIM, (head + 1) * HEAD_DIM)
        query = pack_ref[:rows, cols]
        scores = []
        values = []
        for index, offset in enumerate((0,) + nearby_offsets(seq)):
            values.append(value_refs[index][:, cols])
            score = dot_nt(query, key_refs[index][:, cols]) * (scale * LOG2E)
            if index > 0:
                valid = (seq + offset >= 0) & (seq + offset < blocks)
                score = jnp.where(valid, score, -1e30)
            scores.append(score)
        top = scores[0]
        for score in scores[1:]:
            top = jnp.maximum(top, score)
        top = jnp.max(top, axis=1, keepdims=True)
        total = jnp.zeros((rows, rows), F32)
        mixed = jnp.zeros((rows, HEAD_DIM), F32)
        for score, value in zip(scores, values):
            weight = jnp.exp2(score - top)
            total = total + weight
            mixed = mixed + dot(weight.astype(BF16), value)
        total = jnp.sum(total, axis=1, keepdims=True)
        att_ref[:, cols] = (mixed / total).astype(BF16)
        lse_all = jnp.where(lane == head, top + jnp.log2(total), lse_all)
    lse_ref[...] = lse_all
    pack_ref[rows:, :rows] = stat_rows(lse_all, heads)
    pack_ref[rows:, rows:] = jnp.zeros((STAT_ROWS, width - rows), BF16)


def out_kernel(att_ref, weight_ref, own_ref, other_ref):
    rows, width = own_ref.shape
    for start in range(0, width, OUT_STEP):
        product = dot(att_ref[...], weight_ref[:, start : start + OUT_STEP]).astype(BF16)
        own_ref[:, start : start + OUT_STEP] = product[:rows]
        other_ref[:, start : start + OUT_STEP] = product[rows:]


def lane_sums(values):
    total = values[:, :HEAD_DIM]
    for start in range(HEAD_DIM, values.shape[1], HEAD_DIM):
        total = total + values[:, start : start + HEAD_DIM]
    return total


def norm_kernel(near_ref, far_ref, residual_ref, gain_ref, unit_ref, sigma_ref, normed_ref):
    rows, width = residual_ref.shape
    spans = [slice(at, at + NORM_STEP) for at in range(0, width, NORM_STEP)]
    total = jnp.zeros((rows, HEAD_DIM), F32)
    for cols in spans:
        stream = residual_ref[:, cols].astype(F32) + near_ref[:, cols].astype(F32) + far_ref[:, cols].astype(F32)
        unit_ref[:, cols] = stream
        total = total + lane_sums(stream)
    mean = jnp.sum(total, axis=-1, keepdims=True) / width
    total = jnp.zeros((rows, HEAD_DIM), F32)
    for cols in spans:
        centered = unit_ref[:, cols] - mean
        total = total + lane_sums(centered * centered)
    sigma = jnp.sqrt(jnp.sum(total, axis=-1, keepdims=True) / width + EPSILON)
    sigma_ref[...] = jnp.broadcast_to(sigma, sigma_ref.shape)
    inverse = 1.0 / sigma
    for cols in spans:
        unit = (unit_ref[:, cols] - mean) * inverse
        unit_ref[:, cols] = unit
        normed_ref[:, cols] = (unit * gain_ref[:, cols]).astype(BF16)


def norm_back_kernel(near_ref, far_ref, cot_ref, gain_ref, unit_ref, sigma_ref, low_ref, scaled_ref):
    rows, width = cot_ref.shape
    spans = [slice(at, at + NORM_STEP) for at in range(0, width, NORM_STEP)]
    total = jnp.zeros((rows, HEAD_DIM), F32)
    total_along = jnp.zeros((rows, HEAD_DIM), F32)
    for cols in spans:
        grad = cot_ref[:, cols].astype(F32) + near_ref[:, cols].astype(F32) + far_ref[:, cols].astype(F32)
        scaled = grad * gain_ref[:, cols]
        scaled_ref[:, cols] = scaled
        total = total + lane_sums(scaled)
        total_along = total_along + lane_sums(scaled * unit_ref[:, cols])
    mean = jnp.sum(total, axis=-1, keepdims=True) / width
    along = jnp.sum(total_along, axis=-1, keepdims=True) / width
    inverse = 1.0 / sigma_ref[:, :1]
    for cols in spans:
        grad = (scaled_ref[:, cols] - mean - unit_ref[:, cols] * along) * inverse
        low_ref[:, cols] = grad.astype(BF16)


def gelu_and_slope(v):
    root = math.sqrt(2.0 / math.pi)
    square = v * v
    t = jnp.tanh(v * (root + root * 0.044715 * square))
    plus = 0.5 + 0.5 * t
    slope = plus + 0.5 * v * (1.0 - t * t) * (root + 3.0 * root * 0.044715 * square)
    return v * plus, slope


def ffn_kernel(
    own_ref, near_ref, up_ref, pick_ref, grad_ref, grad_copy_ref, inverse_ref, gain_ref, merged_ref, hidden_grad_ref
):
    rows = jnp.concatenate([own_ref[...], near_ref[...]], axis=0)
    source = dot(rows, up_ref[...])
    high = source.astype(BF16)
    low = (source - high.astype(F32)).astype(BF16)
    copied = (dot(high, pick_ref[...]) + dot(low, pick_ref[...])) * gain_ref[...]
    act_copy, slope_copy = gelu_and_slope(copied)
    act, slope = gelu_and_slope(source)
    back_copy = (grad_copy_ref[...] * slope_copy).astype(BF16)
    hidden_grad_ref[...] = (grad_ref[...] * slope + dot_nt(back_copy, pick_ref[...])).astype(BF16)
    merged = act + dot_nt(act_copy.astype(BF16), pick_ref[...])
    merged_ref[...] = (merged * inverse_ref[...]).astype(BF16)


def back_kernel(hidden_grad_ref, up_ref, own_ref, other_ref):
    rows, width = own_ref.shape
    for start in range(0, width, OUT_STEP):
        product = dot_nt(hidden_grad_ref[...], up_ref[start : start + OUT_STEP]).astype(BF16)
        own_ref[:, start : start + OUT_STEP] = product[:rows]
        other_ref[:, start : start + OUT_STEP] = product[rows:]


def grad_attended_own_kernel(low_ref, weight_ref, grad_ref):
    grad_ref[...] = dot_nt(low_ref[...], weight_ref[...]).astype(BF16)


def grad_attended_kernel(own_ref, near_ref, weight_ref, att_ref, pack_ref, delta_ref):
    rows, width = att_ref.shape
    heads = width // HEAD_DIM
    pack_ref[: rows // 2] = own_ref[...]
    pack_ref[rows // 2 : rows] = dot_nt(near_ref[...], weight_ref[...]).astype(BF16)
    product = pack_ref[:rows].astype(F32) * att_ref[...].astype(F32)
    lane = lax.broadcasted_iota(jnp.int32, (rows, HEAD_DIM), 1)
    delta = jnp.zeros((rows, HEAD_DIM), F32)
    for head in range(heads):
        part = jnp.sum(product[:, head * HEAD_DIM : (head + 1) * HEAD_DIM], axis=1, keepdims=True)
        delta = jnp.where(lane == head, part, delta)
    delta_ref[...] = delta
    pack_ref[rows:, :rows] = stat_rows(delta, heads)
    pack_ref[rows:, rows:] = jnp.zeros((STAT_ROWS, width - rows), BF16)


def grad_query_kernel(scale, place, q_pack, do_pack, lse_ref, delta_ref, *refs):
    key_refs, value_refs, grad_ref = refs[0:10:2], refs[1:10:2], refs[10]
    rows, width = grad_ref.shape
    heads = width // HEAD_DIM
    slab = rows // 4
    seq, blocks, core = place[0], place[1], place[2]
    for head in range(heads):
        cols = slice(head * HEAD_DIM, (head + 1) * HEAD_DIM)
        query, out_grad = q_pack[:rows, cols], do_pack[:rows, cols]
        lse, delta = lse_ref[:, head : head + 1], delta_ref[:, head : head + 1]
        total = jnp.zeros((rows, HEAD_DIM), F32)
        for index, offset in enumerate((0,) + nearby_offsets(seq)):
            key, value = key_refs[index][:, cols], value_refs[index][:, cols]
            score = dot_nt(query, key) * (scale * LOG2E) - lse
            if index > 0:
                valid = (seq + offset >= 0) & (seq + offset < blocks)
                score = jnp.where(valid, score, -1e30)
            grad_score = jnp.exp2(score) * (dot_nt(out_grad, value) - delta)
            total = total + dot(grad_score.astype(BF16), key)
        total = total * scale
        for index, start in enumerate(local_starts(core, rows)):
            grad_ref[pl.ds(start, slab), cols] = total[index * slab : (index + 1) * slab]


def grad_key_value_kernel(scale, count, start, *refs):
    packs, refs = refs[: 2 * count], refs[2 * count :]
    k0, v0 = refs[:2]
    grad_key_ref, grad_value_ref = refs[-2:]
    rows, width = k0.shape
    heads = width // HEAD_DIM
    for head in range(heads):
        cols = slice(head * HEAD_DIM, (head + 1) * HEAD_DIM)
        key, value = k0[:, cols], v0[:, cols]
        grad_key = jnp.zeros((rows, HEAD_DIM), F32)
        grad_value = jnp.zeros((rows, HEAD_DIM), F32)
        for index in range(count):
            q_pack, do_pack = packs[2 * index], packs[2 * index + 1]
            query, out_grad = q_pack[:rows, cols], do_pack[:rows, cols]
            score = dot_nt(key, query) * (scale * LOG2E) - read_stat(q_pack, head, heads, rows)
            weight = jnp.exp2(score)
            grad_value = grad_value + dot(weight.astype(BF16), out_grad)
            grad_score = weight * (dot_nt(value, out_grad) - read_stat(do_pack, head, heads, rows))
            grad_key = grad_key + dot(grad_score.astype(BF16), query)
        grad_key = grad_key * scale
        if not start:
            grad_key = grad_key + refs[2][:, cols]
            grad_value = grad_value + refs[3][:, cols]
        grad_key_ref[:, cols] = grad_key
        grad_value_ref[:, cols] = grad_value


def shards(
    query_heads,
    key_heads,
    value_heads,
    residual,
    out_weight,
    ln_gain,
    up_source,
    down_source,
    copy_gain,
    neuron_source,
    cotangent,
):
    rows, head_width = query_heads.shape
    model_width = residual.shape[1]
    src_width = up_source.shape[1]
    half = rows // 2
    scale = 1.0 / math.sqrt(HEAD_DIM)
    seq = lax.axis_index("seq")
    blocks = lax.axis_size("seq")
    tp_place = lax.axis_index("tp")
    core, chip = tp_place % 2, tp_place // 2
    place = jnp.stack([seq, jnp.full_like(seq, blocks), core]).astype(jnp.int32)

    window = [key_heads, value_heads]
    first = [(swap_block(array, 1), swap_block(array, 0)) for array in (key_heads, value_heads)]
    second = [(swap_block(b, 1), swap_block(a, 0)) for a, b in first]
    for (keys, values) in zip(first[0] + second[0], first[1] + second[1]):
        window += [keys, values]

    attended, q_pack, lse = call(
        functools.partial(attention_kernel, scale),
        (
            shape((rows, head_width), BF16),
            shape((rows + STAT_ROWS, head_width), BF16),
            shape((rows, HEAD_DIM), F32),
        ),
        [SMEM] + [VMEM] * 11,
    )(place, query_heads, *window)

    def two_parts(kernel, operands):
        return call(kernel, (shape((half, model_width), BF16),) * 2, [VMEM, VMEM])(*operands)

    def chip_sum(own, other):
        return own.astype(F32) + swap_core(other).astype(F32)

    near = chip_sum(*two_parts(out_kernel, (attended, out_weight))).astype(BF16)
    far = swap_chip(near)

    def half_rows(array, place):
        split = array.reshape(2, 2, half // 2, array.shape[1])
        return lax.dynamic_slice_in_dim(split, place, 1, 1).reshape(half, array.shape[1])

    cot_own = half_rows(cotangent, core)
    cot_local = jnp.concatenate([cot_own, half_rows(cotangent, 1 - core)], axis=0)
    grad_merged = dot_nt(after(cot_local, near), down_source)

    residual_own = half_rows(residual, core)
    local_source = neuron_source - tp_place * src_width
    pick = (lax.broadcasted_iota(jnp.int32, (src_width, src_width), 0) == local_source[None, :])
    counts = 1.0 + jnp.sum(pick.astype(F32), axis=1)
    pick = pick.astype(BF16)
    inverse = 1.0 / counts
    grad_merged = grad_merged * inverse
    grad_high = grad_merged.astype(BF16)
    grad_rest = (grad_merged - grad_high.astype(F32)).astype(BF16)
    grad_copy = (dot(grad_high, pick) + dot(grad_rest, pick)) * copy_gain
    gain_row = ln_gain.reshape(1, model_width)
    inverse_row = inverse.reshape(1, src_width)
    copy_row = copy_gain.reshape(1, src_width)

    far, pick, grad_merged, grad_copy = lax.optimization_barrier((far, pick, grad_merged, grad_copy))

    far, q_a = lax.optimization_barrier((far, swap_block(after(q_pack, near), 0)))

    unit, sigma, normed = call(
        norm_kernel,
        (
            shape((half, model_width), F32),
            shape((half, HEAD_DIM), F32),
            shape((half, model_width), BF16),
        ),
        [VMEM] * 4,
    )(near, far, residual_own, gain_row)
    near_normed = swap_core(normed)
    merged, hidden_grad = call(ffn_kernel, (shape((rows, src_width), BF16),) * 2, [VMEM] * 8)(
        normed, near_normed, up_source, pick, grad_merged, grad_copy, inverse_row, copy_row
    )
    ffn_parts = two_parts(out_kernel, (merged, down_source))
    hidden_grad, ffn_parts, q_b = lax.optimization_barrier(
        (hidden_grad, ffn_parts, swap_block(after(q_pack, normed), 1))
    )
    near = chip_sum(*two_parts(back_kernel, (hidden_grad, up_source))).astype(BF16)
    far = swap_chip(near)
    ffn_chip = chip_sum(*ffn_parts).reshape(2, half // 2, model_width)
    ffn_send = jnp.where(chip == 0, ffn_chip[1], ffn_chip[0]).astype(BF16)
    ffn_mine = jnp.where(chip == 0, ffn_chip[0], ffn_chip[1])
    q_c = swap_block(after(q_b, near), 0)
    far, ffn_send, ffn_mine, q_c = lax.optimization_barrier((far, ffn_send, ffn_mine, q_c))

    low = call(
        norm_back_kernel,
        shape((half, model_width), BF16),
        [VMEM] * 6,
        scratch=[pltpu.VMEM((half, model_width), F32)],
    )(near, far, cot_own, gain_row, unit, sigma)
    near_low = swap_core(low)
    ffn_far = swap_chip(after(ffn_send, low))
    grad_own = call(grad_attended_own_kernel, shape((half, head_width), BF16), [VMEM] * 2)(low, out_weight)
    near_low, grad_own = lax.optimization_barrier((near_low, grad_own))
    do_pack, delta = call(
        grad_attended_kernel,
        (shape((rows + STAT_ROWS, head_width), BF16), shape((rows, HEAD_DIM), F32)),
        [VMEM] * 4,
    )(grad_own, near_low, out_weight, attended)

    do_a, do_b = swap_block(do_pack, 0), swap_block(do_pack, 1)

    q_d = swap_block(after(q_a, do_pack), 1)
    do_a, do_b, do_own = lax.optimization_barrier((do_a, do_b, do_pack))
    do_c, do_d = swap_block(do_b, 0), swap_block(do_a, 1)
    grad_query = call(
        functools.partial(grad_query_kernel, scale),
        shape((rows, head_width), F32),
        [SMEM] + [VMEM] * 14,
    )(place, q_pack, do_own, lse, delta, *window)

    def grad_key_value(pairs, sums):
        return call(
            functools.partial(grad_key_value_kernel, scale, len(pairs), not sums),
            (shape((rows, head_width), F32),) * 2,
            [VMEM] * (2 * len(pairs) + 2 + len(sums)),
        )(*[pack for pair in pairs for pack in pair], key_heads, value_heads, *sums)

    sums = grad_key_value([(q_pack, do_own), (q_a, do_a), (q_b, do_b)], ())
    own_unit = lax.dynamic_slice_in_dim(unit, chip * (half // 2), half // 2, 0)
    encoded = own_unit * ln_gain + (ffn_mine + after(ffn_far, grad_query, *sums).astype(F32))
    grad_key, grad_value = grad_key_value([(q_c, do_c), (q_d, do_d)], sums)

    col_width = model_width // lax.axis_size("tp")
    first = jnp.where(core == 0, low, near_low).reshape(2, half // 2, model_width)
    second = jnp.where(core == 0, near_low, low).reshape(2, half // 2, model_width)
    low_all = jnp.stack([first, second], axis=1).reshape(rows, model_width)
    grad_residual = lax.dynamic_slice_in_dim(low_all, tp_place * col_width, col_width, 1).astype(F32)
    return (encoded, grad_query, grad_key, grad_value, grad_residual)


def solution(mesh):
    in_specs = (
        P("seq", "tp"),
        P("seq", "tp"),
        P("seq", "tp"),
        P("seq", None),
        P("tp", None),
        P(),
        P(None, "tp"),
        P("tp", None),
        P("tp"),
        P("tp"),
        P("seq", None),
    )
    out_specs = (
        P(("seq", "tp"), None),
        P("seq", "tp"),
        P("seq", "tp"),
        P("seq", "tp"),
        P("seq", "tp"),
    )
    return jax.shard_map(shards, mesh=mesh, in_specs=in_specs, out_specs=out_specs, check_vma=False)
```

```python
import functools
import math

import jax
import jax.numpy as jnp
from jax import lax
from jax.experimental import pallas as pl
from jax.experimental.pallas import tpu as pltpu
from jax.sharding import PartitionSpec as P

HEAD_DIM = 128
EPSILON = 1e-05
LOG2E = math.log2(math.e)
F32 = jnp.float32
BF16 = jnp.bfloat16
NT = (((1,), (1,)), ((), ()))
STAT_ROWS = 16
VMEM_LIMIT = 16 * 1024 * 1024
OUT_STEP = 512
NORM_STEP = 512
COST = 1024

VMEM = pl.BlockSpec(memory_space=pltpu.VMEM)
SMEM = pl.BlockSpec(memory_space=pltpu.SMEM)


def call(kernel, out_shape, in_specs, scratch=()):
    return pl.pallas_call(
        kernel,
        out_shape=out_shape,
        in_specs=in_specs,
        out_specs=jax.tree.map(lambda _: VMEM, out_shape),
        scratch_shapes=list(scratch),
        compiler_params=pltpu.CompilerParams(vmem_limit_bytes=VMEM_LIMIT),
        cost_estimate=pl.CostEstimate(flops=COST, bytes_accessed=COST, transcendentals=0),
    )


def shape(dims, dtype):
    return jax.ShapeDtypeStruct(dims, dtype)


def dot(a, b):
    return jnp.dot(a, b, preferred_element_type=F32)


def dot_nt(a, b):
    return lax.dot_general(a, b, NT, preferred_element_type=F32)


def swap_core(array):
    return lax.ppermute(array, "tp", [(0, 1), (1, 0), (2, 3), (3, 2)])


def swap_chip(array):
    return lax.ppermute(array, "tp", [(0, 2), (2, 0), (1, 3), (3, 1)])


def after(value, *earlier):
    return lax.optimization_barrier((value, earlier))[0]


def swap_block(array, first):
    count = lax.axis_size("seq")
    ahead = [(i, i + 1) for i in range(first, count - 1, 2)]
    return lax.ppermute(array, "seq", ahead + [(j, i) for i, j in ahead])


def nearby_offsets(seq):
    side = 2 * (seq % 2) - 1
    return side, -side, 2 * side, -2 * side


def three_parts(values):
    high = values.astype(BF16).astype(F32)
    middle = (values - high).astype(BF16).astype(F32)
    low = values - high - middle
    return high, middle, low


def stat_rows(columns, heads):
    rows = columns.T[:heads]
    parts = three_parts(rows)
    fill = jnp.zeros((STAT_ROWS - 3 * heads, rows.shape[1]), F32)
    return jnp.concatenate(parts + (fill,), axis=0).astype(BF16)


def read_stat(pack, head, heads, rows):
    block = pack[rows : rows + STAT_ROWS, :rows].astype(F32)
    line = lax.broadcasted_iota(jnp.int32, block.shape, 0)
    chosen = (line % heads == head) & (line < 3 * heads)
    return jnp.sum(jnp.where(chosen, block, 0.0), axis=0, keepdims=True)


def head_columns(head):
    return pl.ds(pl.multiple_of(head * HEAD_DIM, HEAD_DIM), HEAD_DIM)


def pick_lane(columns, lane):
    lanes = lax.broadcasted_iota(jnp.int32, columns.shape, 1)
    return jnp.sum(jnp.where(lanes == lane, columns, 0.0), axis=1, keepdims=True)


def local_starts(core, rows):
    slab = rows // 4
    return [(2 * part + (core if own else 1 - core)) * slab for own in (True, False) for part in range(2)]


def attention_kernel(scale, place, q_ref, *refs):
    key_refs, value_refs = refs[0:10:2], refs[1:10:2]
    att_ref, pack_ref, lse_ref = refs[10:]
    rows, width = q_ref.shape
    heads = width // HEAD_DIM
    slab = rows // 4
    seq, blocks, core = place[0], place[1], place[2]
    for index, start in enumerate(local_starts(core, rows)):
        pack_ref[index * slab : (index + 1) * slab] = q_ref[pl.ds(start, slab)]
    lane = lax.broadcasted_iota(jnp.int32, (rows, HEAD_DIM), 1)
    lse_all = jnp.zeros((rows, HEAD_DIM), F32)
    for head in range(heads):
        cols = slice(head * HEAD_DIM, (head + 1) * HEAD_DIM)
        query = pack_ref[:rows, cols]
        scores = []
        values = []
        for index, offset in enumerate((0,) + nearby_offsets(seq)):
            values.append(value_refs[index][:, cols])
            score = dot_nt(query, key_refs[index][:, cols]) * (scale * LOG2E)
            if index > 0:
                valid = (seq + offset >= 0) & (seq + offset < blocks)
                score = jnp.where(valid, score, -1e30)
            scores.append(score)
        top = scores[0]
        for score in scores[1:]:
            top = jnp.maximum(top, score)
        top = jnp.max(top, axis=1, keepdims=True)
        total = jnp.zeros((rows, rows), F32)
        mixed = jnp.zeros((rows, HEAD_DIM), F32)
        for score, value in zip(scores, values):
            weight = jnp.exp2(score - top)
            total = total + weight
            mixed = mixed + dot(weight.astype(BF16), value)
        total = jnp.sum(total, axis=1, keepdims=True)
        att_ref[:, cols] = (mixed / total).astype(BF16)
        lse_all = jnp.where(lane == head, top + jnp.log2(total), lse_all)
    lse_ref[...] = lse_all
    pack_ref[rows:, :rows] = stat_rows(lse_all, heads)
    pack_ref[rows:, rows:] = jnp.zeros((STAT_ROWS, width - rows), BF16)


def out_kernel(att_ref, weight_ref, own_ref, other_ref):
    rows, width = own_ref.shape
    for start in range(0, width, OUT_STEP):
        product = dot(att_ref[...], weight_ref[:, start : start + OUT_STEP]).astype(BF16)
        own_ref[:, start : start + OUT_STEP] = product[:rows]
        other_ref[:, start : start + OUT_STEP] = product[rows:]


def lane_sums(values):
    total = values[:, :HEAD_DIM]
    for start in range(HEAD_DIM, values.shape[1], HEAD_DIM):
        total = total + values[:, start : start + HEAD_DIM]
    return total


def norm_kernel(near_ref, far_ref, residual_ref, gain_ref, unit_ref, sigma_ref, normed_ref):
    rows, width = residual_ref.shape
    spans = [slice(at, at + NORM_STEP) for at in range(0, width, NORM_STEP)]
    total = jnp.zeros((rows, HEAD_DIM), F32)
    for cols in spans:
        stream = residual_ref[:, cols].astype(F32) + near_ref[:, cols].astype(F32) + far_ref[:, cols].astype(F32)
        unit_ref[:, cols] = stream
        total = total + lane_sums(stream)
    mean = jnp.sum(total, axis=-1, keepdims=True) / width
    total = jnp.zeros((rows, HEAD_DIM), F32)
    for cols in spans:
        centered = unit_ref[:, cols] - mean
        total = total + lane_sums(centered * centered)
    sigma = jnp.sqrt(jnp.sum(total, axis=-1, keepdims=True) / width + EPSILON)
    sigma_ref[...] = jnp.broadcast_to(sigma, sigma_ref.shape)
    inverse = 1.0 / sigma
    for cols in spans:
        unit = (unit_ref[:, cols] - mean) * inverse
        unit_ref[:, cols] = unit
        normed_ref[:, cols] = (unit * gain_ref[:, cols]).astype(BF16)


def norm_back_kernel(near_ref, far_ref, cot_ref, gain_ref, unit_ref, sigma_ref, low_ref, scaled_ref):
    rows, width = cot_ref.shape
    spans = [slice(at, at + NORM_STEP) for at in range(0, width, NORM_STEP)]
    total = jnp.zeros((rows, HEAD_DIM), F32)
    total_along = jnp.zeros((rows, HEAD_DIM), F32)
    for cols in spans:
        grad = cot_ref[:, cols].astype(F32) + near_ref[:, cols].astype(F32) + far_ref[:, cols].astype(F32)
        scaled = grad * gain_ref[:, cols]
        scaled_ref[:, cols] = scaled
        total = total + lane_sums(scaled)
        total_along = total_along + lane_sums(scaled * unit_ref[:, cols])
    mean = jnp.sum(total, axis=-1, keepdims=True) / width
    along = jnp.sum(total_along, axis=-1, keepdims=True) / width
    inverse = 1.0 / sigma_ref[:, :1]
    for cols in spans:
        grad = (scaled_ref[:, cols] - mean - unit_ref[:, cols] * along) * inverse
        low_ref[:, cols] = grad.astype(BF16)


def gelu_and_slope(v):
    root = math.sqrt(2.0 / math.pi)
    square = v * v
    t = jnp.tanh(v * (root + root * 0.044715 * square))
    plus = 0.5 + 0.5 * t
    slope = plus + 0.5 * v * (1.0 - t * t) * (root + 3.0 * root * 0.044715 * square)
    return v * plus, slope


def ffn_kernel(
    own_ref, near_ref, up_ref, pick_ref, grad_ref, grad_copy_ref, inverse_ref, gain_ref, merged_ref, hidden_grad_ref
):
    rows = jnp.concatenate([own_ref[...], near_ref[...]], axis=0)
    source = dot(rows, up_ref[...])
    high = source.astype(BF16)
    low = (source - high.astype(F32)).astype(BF16)
    copied = (dot(high, pick_ref[...]) + dot(low, pick_ref[...])) * gain_ref[...]
    act_copy, slope_copy = gelu_and_slope(copied)
    act, slope = gelu_and_slope(source)
    back_copy = (grad_copy_ref[...] * slope_copy).astype(BF16)
    hidden_grad_ref[...] = (grad_ref[...] * slope + dot_nt(back_copy, pick_ref[...])).astype(BF16)
    merged = act + dot_nt(act_copy.astype(BF16), pick_ref[...])
    merged_ref[...] = (merged * inverse_ref[...]).astype(BF16)


def back_kernel(hidden_grad_ref, up_ref, own_ref, other_ref):
    rows, width = own_ref.shape
    for start in range(0, width, OUT_STEP):
        product = dot_nt(hidden_grad_ref[...], up_ref[start : start + OUT_STEP]).astype(BF16)
        own_ref[:, start : start + OUT_STEP] = product[:rows]
        other_ref[:, start : start + OUT_STEP] = product[rows:]


def grad_attended_own_kernel(low_ref, weight_ref, grad_ref):
    grad_ref[...] = dot_nt(low_ref[...], weight_ref[...]).astype(BF16)


def grad_attended_kernel(own_ref, near_ref, weight_ref, att_ref, pack_ref, delta_ref):
    rows, width = att_ref.shape
    heads = width // HEAD_DIM
    pack_ref[: rows // 2] = own_ref[...]
    pack_ref[rows // 2 : rows] = dot_nt(near_ref[...], weight_ref[...]).astype(BF16)
    product = pack_ref[:rows].astype(F32) * att_ref[...].astype(F32)
    lane = lax.broadcasted_iota(jnp.int32, (rows, HEAD_DIM), 1)
    delta = jnp.zeros((rows, HEAD_DIM), F32)
    for head in range(heads):
        part = jnp.sum(product[:, head * HEAD_DIM : (head + 1) * HEAD_DIM], axis=1, keepdims=True)
        delta = jnp.where(lane == head, part, delta)
    delta_ref[...] = delta
    pack_ref[rows:, :rows] = stat_rows(delta, heads)
    pack_ref[rows:, rows:] = jnp.zeros((STAT_ROWS, width - rows), BF16)


def grad_query_kernel(scale, place, q_pack, do_pack, lse_ref, delta_ref, *refs):
    key_refs, value_refs, grad_ref = refs[0:10:2], refs[1:10:2], refs[10]
    rows, width = grad_ref.shape
    heads = width // HEAD_DIM
    slab = rows // 4
    seq, blocks, core = place[0], place[1], place[2]

    @pl.loop(0, heads)
    def _(head):
        cols = head_columns(head)
        query, out_grad = q_pack[:rows, cols], do_pack[:rows, cols]
        lse, delta = pick_lane(lse_ref[...], head), pick_lane(delta_ref[...], head)
        total = jnp.zeros((rows, HEAD_DIM), F32)
        for index, offset in enumerate((0,) + nearby_offsets(seq)):
            key, value = key_refs[index][:, cols], value_refs[index][:, cols]
            score = dot_nt(query, key) * (scale * LOG2E) - lse
            if index > 0:
                valid = (seq + offset >= 0) & (seq + offset < blocks)
                score = jnp.where(valid, score, -1e30)
            grad_score = jnp.exp2(score) * (dot_nt(out_grad, value) - delta)
            total = total + dot(grad_score.astype(BF16), key)
        total = total * scale
        for index, start in enumerate(local_starts(core, rows)):
            grad_ref[pl.ds(start, slab), cols] = total[index * slab : (index + 1) * slab]


def grad_key_value_kernel(scale, count, start, *refs):
    packs, refs = refs[: 2 * count], refs[2 * count :]
    k0, v0 = refs[:2]
    grad_key_ref, grad_value_ref = refs[-2:]
    rows, width = k0.shape
    heads = width // HEAD_DIM

    for head in range(heads):
        cols = slice(head * HEAD_DIM, (head + 1) * HEAD_DIM)
        key, value = k0[:, cols], v0[:, cols]
        grad_key = jnp.zeros((rows, HEAD_DIM), F32)
        grad_value = jnp.zeros((rows, HEAD_DIM), F32)
        for index in range(count):
            q_pack, do_pack = packs[2 * index], packs[2 * index + 1]
            query, out_grad = q_pack[:rows, cols], do_pack[:rows, cols]
            score = dot_nt(key, query) * (scale * LOG2E) - read_stat(q_pack, head, heads, rows)
            weight = jnp.exp2(score)
            grad_value = grad_value + dot(weight.astype(BF16), out_grad)
            grad_score = weight * (dot_nt(value, out_grad) - read_stat(do_pack, head, heads, rows))
            grad_key = grad_key + dot(grad_score.astype(BF16), query)
        grad_key = grad_key * scale
        if not start:
            grad_key = grad_key + refs[2][:, cols]
            grad_value = grad_value + refs[3][:, cols]
        grad_key_ref[:, cols] = grad_key
        grad_value_ref[:, cols] = grad_value


def shards(
    query_heads,
    key_heads,
    value_heads,
    residual,
    out_weight,
    ln_gain,
    up_source,
    down_source,
    copy_gain,
    neuron_source,
    cotangent,
):
    rows, head_width = query_heads.shape
    model_width = residual.shape[1]
    src_width = up_source.shape[1]
    half = rows // 2
    scale = 1.0 / math.sqrt(HEAD_DIM)
    seq = lax.axis_index("seq")
    blocks = lax.axis_size("seq")
    tp_place = lax.axis_index("tp")
    core, chip = tp_place % 2, tp_place // 2
    place = jnp.stack([seq, jnp.full_like(seq, blocks), core]).astype(jnp.int32)

    window = [key_heads, value_heads]
    first = [(swap_block(array, 1), swap_block(array, 0)) for array in (key_heads, value_heads)]
    second = [(swap_block(b, 1), swap_block(a, 0)) for a, b in first]
    for (keys, values) in zip(first[0] + second[0], first[1] + second[1]):
        window += [keys, values]

    attended, q_pack, lse = call(
        functools.partial(attention_kernel, scale),
        (
            shape((rows, head_width), BF16),
            shape((rows + STAT_ROWS, head_width), BF16),
            shape((rows, HEAD_DIM), F32),
        ),
        [SMEM] + [VMEM] * 11,
    )(place, query_heads, *window)

    def two_parts(kernel, operands):
        return call(kernel, (shape((half, model_width), BF16),) * 2, [VMEM, VMEM])(*operands)

    def chip_sum(own, other):
        return own.astype(F32) + swap_core(other).astype(F32)

    near = chip_sum(*two_parts(out_kernel, (attended, out_weight))).astype(BF16)
    far = swap_chip(near)

    def half_rows(array, place):
        split = array.reshape(2, 2, half // 2, array.shape[1])
        return lax.dynamic_slice_in_dim(split, place, 1, 1).reshape(half, array.shape[1])

    cot_own = half_rows(cotangent, core)
    cot_local = jnp.concatenate([cot_own, half_rows(cotangent, 1 - core)], axis=0)
    grad_merged = dot_nt(after(cot_local, near), down_source)

    residual_own = half_rows(residual, core)
    local_source = neuron_source - tp_place * src_width
    pick = (lax.broadcasted_iota(jnp.int32, (src_width, src_width), 0) == local_source[None, :])
    counts = 1.0 + jnp.sum(pick.astype(F32), axis=1)
    pick = pick.astype(BF16)
    inverse = 1.0 / counts
    grad_merged = grad_merged * inverse
    grad_high = grad_merged.astype(BF16)
    grad_rest = (grad_merged - grad_high.astype(F32)).astype(BF16)
    grad_copy = (dot(grad_high, pick) + dot(grad_rest, pick)) * copy_gain
    gain_row = ln_gain.reshape(1, model_width)
    inverse_row = inverse.reshape(1, src_width)
    copy_row = copy_gain.reshape(1, src_width)

    far, pick, grad_merged, grad_copy = lax.optimization_barrier((far, pick, grad_merged, grad_copy))

    far, q_a = lax.optimization_barrier((far, swap_block(after(q_pack, near), 0)))

    unit, sigma, normed = call(
        norm_kernel,
        (
            shape((half, model_width), F32),
            shape((half, HEAD_DIM), F32),
            shape((half, model_width), BF16),
        ),
        [VMEM] * 4,
    )(near, far, residual_own, gain_row)
    near_normed = swap_core(normed)
    merged, hidden_grad = call(ffn_kernel, (shape((rows, src_width), BF16),) * 2, [VMEM] * 8)(
        normed, near_normed, up_source, pick, grad_merged, grad_copy, inverse_row, copy_row
    )
    ffn_parts = two_parts(out_kernel, (merged, down_source))
    hidden_grad, ffn_parts, q_b = lax.optimization_barrier(
        (hidden_grad, ffn_parts, swap_block(after(q_pack, normed), 1))
    )
    near = chip_sum(*two_parts(back_kernel, (hidden_grad, up_source))).astype(BF16)
    far = swap_chip(near)
    ffn_chip = chip_sum(*ffn_parts).reshape(2, half // 2, model_width)
    ffn_send = jnp.where(chip == 0, ffn_chip[1], ffn_chip[0]).astype(BF16)
    ffn_mine = jnp.where(chip == 0, ffn_chip[0], ffn_chip[1])
    q_c = swap_block(after(q_b, near), 0)
    far, ffn_send, ffn_mine, q_c = lax.optimization_barrier((far, ffn_send, ffn_mine, q_c))

    low = call(
        norm_back_kernel,
        shape((half, model_width), BF16),
        [VMEM] * 6,
        scratch=[pltpu.VMEM((half, model_width), F32)],
    )(near, far, cot_own, gain_row, unit, sigma)
    near_low = swap_core(low)
    ffn_far = swap_chip(after(ffn_send, low))
    grad_own = call(grad_attended_own_kernel, shape((half, head_width), BF16), [VMEM] * 2)(low, out_weight)
    near_low, grad_own = lax.optimization_barrier((near_low, grad_own))
    do_pack, delta = call(
        grad_attended_kernel,
        (shape((rows + STAT_ROWS, head_width), BF16), shape((rows, HEAD_DIM), F32)),
        [VMEM] * 4,
    )(grad_own, near_low, out_weight, attended)

    do_a, do_b = swap_block(do_pack, 0), swap_block(do_pack, 1)

    q_d = swap_block(after(q_a, do_pack), 1)
    do_a, do_b, do_own = lax.optimization_barrier((do_a, do_b, do_pack))
    do_c, do_d = swap_block(do_b, 0), swap_block(do_a, 1)
    grad_query = call(
        functools.partial(grad_query_kernel, scale),
        shape((rows, head_width), F32),
        [SMEM] + [VMEM] * 14,
    )(place, q_pack, do_own, lse, delta, *window)

    def grad_key_value(pairs, sums):
        return call(
            functools.partial(grad_key_value_kernel, scale, len(pairs), not sums),
            (shape((rows, head_width), F32),) * 2,
            [VMEM] * (2 * len(pairs) + 2 + len(sums)),
        )(*[pack for pair in pairs for pack in pair], key_heads, value_heads, *sums)

    sums = grad_key_value([(q_pack, do_own), (q_a, do_a), (q_b, do_b)], ())
    own_unit = lax.dynamic_slice_in_dim(unit, chip * (half // 2), half // 2, 0)
    encoded = own_unit * ln_gain + (ffn_mine + after(ffn_far, grad_query, *sums).astype(F32))
    grad_key, grad_value = grad_key_value([(q_c, do_c), (q_d, do_d)], sums)

    col_width = model_width // lax.axis_size("tp")
    first = jnp.where(core == 0, low, near_low).reshape(2, half // 2, model_width)
    second = jnp.where(core == 0, near_low, low).reshape(2, half // 2, model_width)
    low_all = jnp.stack([first, second], axis=1).reshape(rows, model_width)
    grad_residual = lax.dynamic_slice_in_dim(low_all, tp_place * col_width, col_width, 1).astype(F32)
    return (encoded, grad_query, grad_key, grad_value, grad_residual)


def solution(mesh):
    in_specs = (
        P("seq", "tp"),
        P("seq", "tp"),
        P("seq", "tp"),
        P("seq", None),
        P("tp", None),
        P(),
        P(None, "tp"),
        P("tp", None),
        P("tp"),
        P("tp"),
        P("seq", None),
    )
    out_specs = (
        P(("seq", "tp"), None),
        P("seq", "tp"),
        P("seq", "tp"),
        P("seq", "tp"),
        P("seq", "tp"),
    )
    return jax.shard_map(shards, mesh=mesh, in_specs=in_specs, out_specs=out_specs, check_vma=False)
```

```python
import functools
import math

import jax
import jax.numpy as jnp
from jax import lax
from jax.experimental import pallas as pl
from jax.experimental.pallas import tpu as pltpu
from jax.sharding import PartitionSpec as P

HEAD_DIM = 128
EPSILON = 1e-05
LOG2E = math.log2(math.e)
F32 = jnp.float32
BF16 = jnp.bfloat16
NT = (((1,), (1,)), ((), ()))
STAT_ROWS = 16
VMEM_LIMIT = 16 * 1024 * 1024
OUT_STEP = 512
NORM_STEP = 512
COST = 1024

VMEM = pl.BlockSpec(memory_space=pltpu.VMEM)
SMEM = pl.BlockSpec(memory_space=pltpu.SMEM)


def call(kernel, out_shape, in_specs, scratch=()):
    return pl.pallas_call(
        kernel,
        out_shape=out_shape,
        in_specs=in_specs,
        out_specs=jax.tree.map(lambda _: VMEM, out_shape),
        scratch_shapes=list(scratch),
        compiler_params=pltpu.CompilerParams(vmem_limit_bytes=VMEM_LIMIT),
        cost_estimate=pl.CostEstimate(flops=COST, bytes_accessed=COST, transcendentals=0),
    )


def shape(dims, dtype):
    return jax.ShapeDtypeStruct(dims, dtype)


def dot(a, b):
    return jnp.dot(a, b, preferred_element_type=F32)


def dot_nt(a, b):
    return lax.dot_general(a, b, NT, preferred_element_type=F32)


def swap_core(array):
    return lax.ppermute(array, "tp", [(0, 1), (1, 0), (2, 3), (3, 2)])


def swap_chip(array):
    return lax.ppermute(array, "tp", [(0, 2), (2, 0), (1, 3), (3, 1)])


def after(value, *earlier):
    return lax.optimization_barrier((value, earlier))[0]


def swap_block(array, first):
    count = lax.axis_size("seq")
    ahead = [(i, i + 1) for i in range(first, count - 1, 2)]
    return lax.ppermute(array, "seq", ahead + [(j, i) for i, j in ahead])


def nearby_offsets(seq):
    side = 2 * (seq % 2) - 1
    return side, -side, 2 * side, -2 * side


def three_parts(values):
    high = values.astype(BF16).astype(F32)
    middle = (values - high).astype(BF16).astype(F32)
    low = values - high - middle
    return high, middle, low


def stat_rows(columns, heads):
    rows = columns.T[:heads]
    parts = three_parts(rows)
    fill = jnp.zeros((STAT_ROWS - 3 * heads, rows.shape[1]), F32)
    return jnp.concatenate(parts + (fill,), axis=0).astype(BF16)


def read_stat(pack, head, heads, rows):
    block = pack[rows : rows + STAT_ROWS, :rows].astype(F32)
    line = lax.broadcasted_iota(jnp.int32, block.shape, 0)
    chosen = (line % heads == head) & (line < 3 * heads)
    return jnp.sum(jnp.where(chosen, block, 0.0), axis=0, keepdims=True)


def head_columns(head):
    return pl.ds(pl.multiple_of(head * HEAD_DIM, HEAD_DIM), HEAD_DIM)


def pick_lane(columns, lane):
    lanes = lax.broadcasted_iota(jnp.int32, columns.shape, 1)
    return jnp.sum(jnp.where(lanes == lane, columns, 0.0), axis=1, keepdims=True)


def local_starts(core, rows):
    slab = rows // 4
    return [(2 * part + (core if own else 1 - core)) * slab for own in (True, False) for part in range(2)]


def attention_kernel(scale, place, q_ref, *refs):
    key_refs, value_refs = refs[0:10:2], refs[1:10:2]
    att_ref, pack_ref, lse_ref = refs[10:]
    rows, width = q_ref.shape
    heads = width // HEAD_DIM
    slab = rows // 4
    seq, blocks, core = place[0], place[1], place[2]
    for index, start in enumerate(local_starts(core, rows)):
        pack_ref[index * slab : (index + 1) * slab] = q_ref[pl.ds(start, slab)]
    lane = lax.broadcasted_iota(jnp.int32, (rows, HEAD_DIM), 1)
    lse_all = jnp.zeros((rows, HEAD_DIM), F32)
    for head in range(heads):
        cols = slice(head * HEAD_DIM, (head + 1) * HEAD_DIM)
        query = pack_ref[:rows, cols]
        scores = []
        values = []
        for index, offset in enumerate((0,) + nearby_offsets(seq)):
            values.append(value_refs[index][:, cols])
            score = dot_nt(query, key_refs[index][:, cols]) * (scale * LOG2E)
            if index > 0:
                valid = (seq + offset >= 0) & (seq + offset < blocks)
                score = jnp.where(valid, score, -1e30)
            scores.append(score)
        top = scores[0]
        for score in scores[1:]:
            top = jnp.maximum(top, score)
        top = jnp.max(top, axis=1, keepdims=True)
        total = jnp.zeros((rows, rows), F32)
        mixed = jnp.zeros((rows, HEAD_DIM), F32)
        for score, value in zip(scores, values):
            weight = jnp.exp2(score - top)
            total = total + weight
            mixed = mixed + dot(weight.astype(BF16), value)
        total = jnp.sum(total, axis=1, keepdims=True)
        att_ref[:, cols] = (mixed / total).astype(BF16)
        lse_all = jnp.where(lane == head, top + jnp.log2(total), lse_all)
    lse_ref[...] = lse_all
    pack_ref[rows:, :rows] = stat_rows(lse_all, heads)
    pack_ref[rows:, rows:] = jnp.zeros((STAT_ROWS, width - rows), BF16)


def out_kernel(att_ref, weight_ref, own_ref, other_ref):
    rows, width = own_ref.shape
    for start in range(0, width, OUT_STEP):
        product = dot(att_ref[...], weight_ref[:, start : start + OUT_STEP]).astype(BF16)
        own_ref[:, start : start + OUT_STEP] = product[:rows]
        other_ref[:, start : start + OUT_STEP] = product[rows:]


def lane_sums(values):
    total = values[:, :HEAD_DIM]
    for start in range(HEAD_DIM, values.shape[1], HEAD_DIM):
        total = total + values[:, start : start + HEAD_DIM]
    return total


def norm_kernel(near_ref, far_ref, residual_ref, gain_ref, unit_ref, sigma_ref, normed_ref):
    rows, width = residual_ref.shape
    spans = [slice(at, at + NORM_STEP) for at in range(0, width, NORM_STEP)]
    total = jnp.zeros((rows, HEAD_DIM), F32)
    for cols in spans:
        stream = residual_ref[:, cols].astype(F32) + near_ref[:, cols].astype(F32) + far_ref[:, cols].astype(F32)
        unit_ref[:, cols] = stream
        total = total + lane_sums(stream)
    mean = jnp.sum(total, axis=-1, keepdims=True) / width
    total = jnp.zeros((rows, HEAD_DIM), F32)
    for cols in spans:
        centered = unit_ref[:, cols] - mean
        total = total + lane_sums(centered * centered)
    sigma = jnp.sqrt(jnp.sum(total, axis=-1, keepdims=True) / width + EPSILON)
    sigma_ref[...] = jnp.broadcast_to(sigma, sigma_ref.shape)
    inverse = 1.0 / sigma
    for cols in spans:
        unit = (unit_ref[:, cols] - mean) * inverse
        unit_ref[:, cols] = unit
        normed_ref[:, cols] = (unit * gain_ref[:, cols]).astype(BF16)


def norm_back_kernel(near_ref, far_ref, cot_ref, gain_ref, unit_ref, sigma_ref, low_ref, scaled_ref):
    rows, width = cot_ref.shape
    spans = [slice(at, at + NORM_STEP) for at in range(0, width, NORM_STEP)]
    total = jnp.zeros((rows, HEAD_DIM), F32)
    total_along = jnp.zeros((rows, HEAD_DIM), F32)
    for cols in spans:
        grad = cot_ref[:, cols].astype(F32) + near_ref[:, cols].astype(F32) + far_ref[:, cols].astype(F32)
        scaled = grad * gain_ref[:, cols]
        scaled_ref[:, cols] = scaled
        total = total + lane_sums(scaled)
        total_along = total_along + lane_sums(scaled * unit_ref[:, cols])
    mean = jnp.sum(total, axis=-1, keepdims=True) / width
    along = jnp.sum(total_along, axis=-1, keepdims=True) / width
    inverse = 1.0 / sigma_ref[:, :1]
    for cols in spans:
        grad = (scaled_ref[:, cols] - mean - unit_ref[:, cols] * along) * inverse
        low_ref[:, cols] = grad.astype(BF16)


def gelu_and_slope(v):
    root = math.sqrt(2.0 / math.pi)
    square = v * v
    t = jnp.tanh(v * (root + root * 0.044715 * square))
    plus = 0.5 + 0.5 * t
    slope = plus + 0.5 * v * (1.0 - t * t) * (root + 3.0 * root * 0.044715 * square)
    return v * plus, slope


def ffn_kernel(
    own_ref, near_ref, up_ref, pick_ref, grad_ref, grad_copy_ref, inverse_ref, gain_ref, merged_ref, hidden_grad_ref
):
    rows = jnp.concatenate([own_ref[...], near_ref[...]], axis=0)
    source = dot(rows, up_ref[...])
    high = source.astype(BF16)
    low = (source - high.astype(F32)).astype(BF16)
    copied = (dot(high, pick_ref[...]) + dot(low, pick_ref[...])) * gain_ref[...]
    act_copy, slope_copy = gelu_and_slope(copied)
    act, slope = gelu_and_slope(source)
    back_copy = (grad_copy_ref[...] * slope_copy).astype(BF16)
    hidden_grad_ref[...] = (grad_ref[...] * slope + dot_nt(back_copy, pick_ref[...])).astype(BF16)
    merged = act + dot_nt(act_copy.astype(BF16), pick_ref[...])
    merged_ref[...] = (merged * inverse_ref[...]).astype(BF16)


def back_kernel(hidden_grad_ref, up_ref, own_ref, other_ref):
    rows, width = own_ref.shape
    for start in range(0, width, OUT_STEP):
        product = dot_nt(hidden_grad_ref[...], up_ref[start : start + OUT_STEP]).astype(BF16)
        own_ref[:, start : start + OUT_STEP] = product[:rows]
        other_ref[:, start : start + OUT_STEP] = product[rows:]


def grad_attended_own_kernel(low_ref, weight_ref, grad_ref):
    grad_ref[...] = dot_nt(low_ref[...], weight_ref[...]).astype(BF16)


def grad_attended_kernel(own_ref, near_ref, weight_ref, att_ref, pack_ref, delta_ref):
    rows, width = att_ref.shape
    heads = width // HEAD_DIM
    pack_ref[: rows // 2] = own_ref[...]
    pack_ref[rows // 2 : rows] = dot_nt(near_ref[...], weight_ref[...]).astype(BF16)
    product = pack_ref[:rows].astype(F32) * att_ref[...].astype(F32)
    lane = lax.broadcasted_iota(jnp.int32, (rows, HEAD_DIM), 1)
    delta = jnp.zeros((rows, HEAD_DIM), F32)
    for head in range(heads):
        part = jnp.sum(product[:, head * HEAD_DIM : (head + 1) * HEAD_DIM], axis=1, keepdims=True)
        delta = jnp.where(lane == head, part, delta)
    delta_ref[...] = delta
    pack_ref[rows:, :rows] = stat_rows(delta, heads)
    pack_ref[rows:, rows:] = jnp.zeros((STAT_ROWS, width - rows), BF16)


def grad_query_kernel(scale, place, q_pack, do_pack, lse_ref, delta_ref, *refs):
    key_refs, value_refs, grad_ref = refs[0:10:2], refs[1:10:2], refs[10]
    rows, width = grad_ref.shape
    heads = width // HEAD_DIM
    slab = rows // 4
    seq, blocks, core = place[0], place[1], place[2]

    @pl.loop(0, heads, unroll=2)
    def _(head):
        cols = head_columns(head)
        query, out_grad = q_pack[:rows, cols], do_pack[:rows, cols]
        lse, delta = pick_lane(lse_ref[...], head), pick_lane(delta_ref[...], head)
        total = jnp.zeros((rows, HEAD_DIM), F32)
        for index, offset in enumerate((0,) + nearby_offsets(seq)):
            key, value = key_refs[index][:, cols], value_refs[index][:, cols]
            score = dot_nt(query, key) * (scale * LOG2E) - lse
            if index > 0:
                valid = (seq + offset >= 0) & (seq + offset < blocks)
                score = jnp.where(valid, score, -1e30)
            grad_score = jnp.exp2(score) * (dot_nt(out_grad, value) - delta)
            total = total + dot(grad_score.astype(BF16), key)
        total = total * scale
        for index, start in enumerate(local_starts(core, rows)):
            grad_ref[pl.ds(start, slab), cols] = total[index * slab : (index + 1) * slab]


def grad_key_value_kernel(scale, count, start, *refs):
    packs, refs = refs[: 2 * count], refs[2 * count :]
    k0, v0 = refs[:2]
    grad_key_ref, grad_value_ref = refs[-2:]
    rows, width = k0.shape
    heads = width // HEAD_DIM

    for head in range(heads):
        cols = slice(head * HEAD_DIM, (head + 1) * HEAD_DIM)
        key, value = k0[:, cols], v0[:, cols]
        grad_key = jnp.zeros((rows, HEAD_DIM), F32)
        grad_value = jnp.zeros((rows, HEAD_DIM), F32)
        for index in range(count):
            q_pack, do_pack = packs[2 * index], packs[2 * index + 1]
            query, out_grad = q_pack[:rows, cols], do_pack[:rows, cols]
            score = dot_nt(key, query) * (scale * LOG2E) - read_stat(q_pack, head, heads, rows)
            weight = jnp.exp2(score)
            grad_value = grad_value + dot(weight.astype(BF16), out_grad)
            grad_score = weight * (dot_nt(value, out_grad) - read_stat(do_pack, head, heads, rows))
            grad_key = grad_key + dot(grad_score.astype(BF16), query)
        grad_key = grad_key * scale
        if not start:
            grad_key = grad_key + refs[2][:, cols]
            grad_value = grad_value + refs[3][:, cols]
        grad_key_ref[:, cols] = grad_key
        grad_value_ref[:, cols] = grad_value


def shards(
    query_heads,
    key_heads,
    value_heads,
    residual,
    out_weight,
    ln_gain,
    up_source,
    down_source,
    copy_gain,
    neuron_source,
    cotangent,
):
    rows, head_width = query_heads.shape
    model_width = residual.shape[1]
    src_width = up_source.shape[1]
    half = rows // 2
    scale = 1.0 / math.sqrt(HEAD_DIM)
    seq = lax.axis_index("seq")
    blocks = lax.axis_size("seq")
    tp_place = lax.axis_index("tp")
    core, chip = tp_place % 2, tp_place // 2
    place = jnp.stack([seq, jnp.full_like(seq, blocks), core]).astype(jnp.int32)

    window = [key_heads, value_heads]
    first = [(swap_block(array, 1), swap_block(array, 0)) for array in (key_heads, value_heads)]
    second = [(swap_block(b, 1), swap_block(a, 0)) for a, b in first]
    for (keys, values) in zip(first[0] + second[0], first[1] + second[1]):
        window += [keys, values]

    attended, q_pack, lse = call(
        functools.partial(attention_kernel, scale),
        (
            shape((rows, head_width), BF16),
            shape((rows + STAT_ROWS, head_width), BF16),
            shape((rows, HEAD_DIM), F32),
        ),
        [SMEM] + [VMEM] * 11,
    )(place, query_heads, *window)

    def two_parts(kernel, operands):
        return call(kernel, (shape((half, model_width), BF16),) * 2, [VMEM, VMEM])(*operands)

    def chip_sum(own, other):
        return own.astype(F32) + swap_core(other).astype(F32)

    near = chip_sum(*two_parts(out_kernel, (attended, out_weight))).astype(BF16)
    far = swap_chip(near)

    def half_rows(array, place):
        split = array.reshape(2, 2, half // 2, array.shape[1])
        return lax.dynamic_slice_in_dim(split, place, 1, 1).reshape(half, array.shape[1])

    cot_own = half_rows(cotangent, core)
    cot_local = jnp.concatenate([cot_own, half_rows(cotangent, 1 - core)], axis=0)
    grad_merged = dot_nt(after(cot_local, near), down_source)

    residual_own = half_rows(residual, core)
    local_source = neuron_source - tp_place * src_width
    pick = (lax.broadcasted_iota(jnp.int32, (src_width, src_width), 0) == local_source[None, :])
    counts = 1.0 + jnp.sum(pick.astype(F32), axis=1)
    pick = pick.astype(BF16)
    inverse = 1.0 / counts
    grad_merged = grad_merged * inverse
    grad_high = grad_merged.astype(BF16)
    grad_rest = (grad_merged - grad_high.astype(F32)).astype(BF16)
    grad_copy = (dot(grad_high, pick) + dot(grad_rest, pick)) * copy_gain
    gain_row = ln_gain.reshape(1, model_width)
    inverse_row = inverse.reshape(1, src_width)
    copy_row = copy_gain.reshape(1, src_width)

    far, pick, grad_merged, grad_copy = lax.optimization_barrier((far, pick, grad_merged, grad_copy))

    far, q_a = lax.optimization_barrier((far, swap_block(after(q_pack, near), 0)))

    unit, sigma, normed = call(
        norm_kernel,
        (
            shape((half, model_width), F32),
            shape((half, HEAD_DIM), F32),
            shape((half, model_width), BF16),
        ),
        [VMEM] * 4,
    )(near, far, residual_own, gain_row)
    near_normed = swap_core(normed)
    merged, hidden_grad = call(ffn_kernel, (shape((rows, src_width), BF16),) * 2, [VMEM] * 8)(
        normed, near_normed, up_source, pick, grad_merged, grad_copy, inverse_row, copy_row
    )
    ffn_parts = two_parts(out_kernel, (merged, down_source))
    hidden_grad, ffn_parts, q_b = lax.optimization_barrier(
        (hidden_grad, ffn_parts, swap_block(after(q_pack, normed), 1))
    )
    near = chip_sum(*two_parts(back_kernel, (hidden_grad, up_source))).astype(BF16)
    far = swap_chip(near)
    ffn_chip = chip_sum(*ffn_parts).reshape(2, half // 2, model_width)
    ffn_send = jnp.where(chip == 0, ffn_chip[1], ffn_chip[0]).astype(BF16)
    ffn_mine = jnp.where(chip == 0, ffn_chip[0], ffn_chip[1])
    q_c = swap_block(after(q_b, near), 0)
    far, ffn_send, ffn_mine, q_c = lax.optimization_barrier((far, ffn_send, ffn_mine, q_c))

    low = call(
        norm_back_kernel,
        shape((half, model_width), BF16),
        [VMEM] * 6,
        scratch=[pltpu.VMEM((half, model_width), F32)],
    )(near, far, cot_own, gain_row, unit, sigma)
    near_low = swap_core(low)
    ffn_far = swap_chip(after(ffn_send, low))
    grad_own = call(grad_attended_own_kernel, shape((half, head_width), BF16), [VMEM] * 2)(low, out_weight)
    near_low, grad_own = lax.optimization_barrier((near_low, grad_own))
    do_pack, delta = call(
        grad_attended_kernel,
        (shape((rows + STAT_ROWS, head_width), BF16), shape((rows, HEAD_DIM), F32)),
        [VMEM] * 4,
    )(grad_own, near_low, out_weight, attended)

    do_a, do_b = swap_block(do_pack, 0), swap_block(do_pack, 1)

    q_d = swap_block(after(q_a, do_pack), 1)
    do_a, do_b, do_own = lax.optimization_barrier((do_a, do_b, do_pack))
    do_c, do_d = swap_block(do_b, 0), swap_block(do_a, 1)
    grad_query = call(
        functools.partial(grad_query_kernel, scale),
        shape((rows, head_width), F32),
        [SMEM] + [VMEM] * 14,
    )(place, q_pack, do_own, lse, delta, *window)

    def grad_key_value(pairs, sums):
        return call(
            functools.partial(grad_key_value_kernel, scale, len(pairs), not sums),
            (shape((rows, head_width), F32),) * 2,
            [VMEM] * (2 * len(pairs) + 2 + len(sums)),
        )(*[pack for pair in pairs for pack in pair], key_heads, value_heads, *sums)

    sums = grad_key_value([(q_pack, do_own), (q_a, do_a), (q_b, do_b)], ())
    own_unit = lax.dynamic_slice_in_dim(unit, chip * (half // 2), half // 2, 0)
    encoded = own_unit * ln_gain + (ffn_mine + after(ffn_far, grad_query, *sums).astype(F32))
    grad_key, grad_value = grad_key_value([(q_c, do_c), (q_d, do_d)], sums)

    col_width = model_width // lax.axis_size("tp")
    first = jnp.where(core == 0, low, near_low).reshape(2, half // 2, model_width)
    second = jnp.where(core == 0, near_low, low).reshape(2, half // 2, model_width)
    low_all = jnp.stack([first, second], axis=1).reshape(rows, model_width)
    grad_residual = lax.dynamic_slice_in_dim(low_all, tp_place * col_width, col_width, 1).astype(F32)
    return (encoded, grad_query, grad_key, grad_value, grad_residual)


def solution(mesh):
    in_specs = (
        P("seq", "tp"),
        P("seq", "tp"),
        P("seq", "tp"),
        P("seq", None),
        P("tp", None),
        P(),
        P(None, "tp"),
        P("tp", None),
        P("tp"),
        P("tp"),
        P("seq", None),
    )
    out_specs = (
        P(("seq", "tp"), None),
        P("seq", "tp"),
        P("seq", "tp"),
        P("seq", "tp"),
        P("seq", "tp"),
    )
    return jax.shard_map(shards, mesh=mesh, in_specs=in_specs, out_specs=out_specs, check_vma=False)
```
